256 devices in a mesh: seq: 64 (over x, z_lo, y, core), cfg: 4 (over z_hi).
Axes of the slice: x: 4, y: 4, z: 8 (z_hi: 4, z_lo: 2; z = z_hi * 2 + z_lo), core: 2. Of those that a mesh axis runs over, the one named last changes fastest.
Arguments:
- hidden: bfloat16 [131072, 1024], P(('seq', 'cfg')), may hold values from -6 to 6
- latent: float32 [80, 65536], P(None, 'seq'), may hold values from -6 to 6
- prompt_mel: float32 [80, 65536], P(None, 'seq'), may hold values from -6 to 6
- window_back: int32 [2048], P('seq'), may hold values from 0 to 4, as said below
- window_ahead: int32 [2048], P('seq'), may hold values from 0 to 4, as said below
- step_index: int32 [1], replicated, may hold values from 8 to 31
- proj_weight: bfloat16 [1024, 80], replicated, may hold values from -0.1875 to 0.1875
- latent_weight: bfloat16 [80, 1024], replicated, may hold values from -0.625 to 0.625
- prompt_weight: bfloat16 [80, 1024], replicated, may hold values from -0.625 to 0.625
- time_weight: bfloat16 [256, 3072], replicated, may hold values from -0.375 to 0.375
- qkv_weight: bfloat16 [1024, 3072], replicated
- attn_out_weight: bfloat16 [1024, 1024], replicated, may hold values from -0.1875 to 0.1875
Outputs:
- latent_next: float32 [80, 65536], P(None, ('seq', 'cfg'))
- hidden_next: bfloat16 [131072, 1024], P(('seq', 'cfg'))
The draws below stay inside these ranges and needn't reach their ends.
Inputs may be any that keep to these rules, and one draw needn't show every extreme that they name: `window_back`: lookback of each block, in blocks of 32 frames; some block takes 4. `window_ahead`: advance of each block, in blocks of 32 frames; some block takes 4.
All inputs are finite; a program needn't handle non-finite values.
Results may differ from the reference program's by a relative error of at most 0.0065.
Values may be sent and summed in bfloat16 or wider, within the bound.
No kernel may reach another device: no remote copies, remote signals or barrier semaphores. Data moves between devices by JAX's collectives and lax.ppermute only.
A program may use at most 64 MiB of HBM per device.

```python
import math
import jax
import jax.numpy as jnp
from jax import lax

D = 1024
HEADS = 16
MEL = 80
FREQ = 256
FR = 512
BLK = 32
MAXB = 4
NSTEPS = 32
HALO = 128
FRAMES = 65536
NBLOCKS = 2048


def window_counts(key):
    first, second = jax.random.split(key)
    counts = jax.random.randint(first, (NBLOCKS,), 0, MAXB + 1)
    spot = jax.random.randint(second, (), 0, NBLOCKS)
    return jnp.where(jnp.arange(NBLOCKS) == spot, MAXB, counts).astype(jnp.int32)


def draw_window_back(key, part):
    key = jax.random.fold_in(key, 3)
    return window_counts(key)


def draw_window_ahead(key, part):
    key = jax.random.fold_in(key, 5)
    return window_counts(key)


def draw_qkv_weight(key, part):
    key = jax.random.fold_in(key, 11)
    first, second, third = jax.random.split(key, 3)
    query = jax.random.normal(first, (D, D), jnp.float32) / jnp.sqrt(jnp.float32(D))
    keyed = jax.random.normal(second, (D, D), jnp.float32) / jnp.sqrt(jnp.float32(D))
    valued = jax.random.normal(third, (D, D), jnp.float32) / jnp.sqrt(jnp.float32(D))
    return jnp.concatenate([query, keyed, valued], axis=1).astype(jnp.bfloat16)


def levels(own_key, shape, cuts, least, top_value):
    factor_of, own = 1.0, jax.random.fold_in(own_key, 6)
    for position, parts in cuts:
        heights = jnp.exp(jax.random.uniform(jax.random.fold_in(own, position), (parts,), jnp.float32, least / len(cuts), top_value / len(cuts)))
        factor_of = factor_of * jnp.repeat(heights, shape[position] // parts).reshape([-1 if axis == position else 1 for axis in range(len(shape))])
    return factor_of


def normal_values(key, shape, deviation, reach, shards=(), kind=jnp.bfloat16):
    array = jax.random.normal(key, shape, jnp.float32) * deviation
    if len(shards) > 0:
        array = levels(key, shape, shards, -0.22, 0.18) * array
    return jnp.clip(array, min=-reach, max=reach).astype(kind)


def setup_inputs(seed: int = 0) -> dict:
    key_of = jax.random.split(jax.random.key(seed), 13)
    hidden = normal_values(key_of[0], (2 * FRAMES, D), 1.0, 6.0, ((0, 256),))
    latent = normal_values(key_of[1], (MEL, FRAMES), 1.0, 6.0, ((1, 64),), jnp.float32)
    prompt_mel = normal_values(key_of[2], (MEL, FRAMES), 1.0, 6.0, ((1, 64),), jnp.float32)
    window_back = draw_window_back(jax.random.fold_in(key_of[12], 71), 0)
    window_ahead = draw_window_ahead(jax.random.fold_in(key_of[12], 71), 0)
    step_index = jax.random.randint(key_of[5], (1,), 8, NSTEPS).astype(jnp.int32)
    proj_weight = normal_values(key_of[6], (D, MEL), D ** -0.5, 0.1875)
    latent_weight = normal_values(key_of[7], (MEL, D), MEL ** -0.5, 0.625)
    prompt_weight = normal_values(key_of[8], (MEL, D), MEL ** -0.5, 0.625)
    time_weight = normal_values(key_of[9], (FREQ, 3 * D), FREQ ** -0.5, 0.375)
    qkv_weight = draw_qkv_weight(jax.random.fold_in(key_of[12], 71), 0)
    attn_out_weight = normal_values(key_of[11], (D, D), D ** -0.5, 0.1875)
    return dict(hidden=hidden, latent=latent, prompt_mel=prompt_mel, window_back=window_back, window_ahead=window_ahead, step_index=step_index, proj_weight=proj_weight, latent_weight=latent_weight, prompt_weight=prompt_weight, time_weight=time_weight, qkv_weight=qkv_weight, attn_out_weight=attn_out_weight)


EPS = 1e-06
GUIDE = 0.5

def layer_norm(rows):
    mean = lax.optimization_barrier(jnp.mean(rows, axis=-1, keepdims=True))
    centered = rows - mean
    spread = lax.optimization_barrier(jnp.mean(centered * centered, axis=-1, keepdims=True))
    return centered * lax.rsqrt(spread + EPS)

def time_value(step):
    return 1.0 - jnp.cos(0.5 * math.pi * step.astype(jnp.float32) / NSTEPS)

def modulation(step_index, time_weight):
    later = time_value(step_index[0] + 1)
    half_freq = time_weight.shape[0] // 2
    freqs = jnp.exp(-math.log(10000.0) * jnp.arange(half_freq, dtype=jnp.float32) / half_freq)
    angles = 1000.0 * later * freqs
    features = jnp.concatenate([jnp.sin(angles), jnp.cos(angles)])
    mixed = jnp.dot(features[None, :], time_weight.astype(jnp.float32), precision=lax.Precision.HIGHEST)[0]
    width = mixed.shape[0] // 3
    return (mixed[:width], mixed[width:2 * width], mixed[2 * width:])

def embed_rows(latent_cols, prompt_cols, flag, latent_weight, prompt_weight):
    dims = (((0,), (0,)), ((), ()))
    base = lax.dot_general(latent_cols, latent_weight.astype(jnp.float32), dims, precision=lax.Precision.HIGHEST)
    extra = lax.dot_general(prompt_cols, prompt_weight.astype(jnp.float32), dims, precision=lax.Precision.HIGHEST)
    return base + flag * extra

def attention_input(first, shift, scale, qkv_weight):
    normed = (layer_norm(first) * (1.0 + scale) + shift).astype(jnp.bfloat16)
    return jnp.dot(normed, qkv_weight, preferred_element_type=jnp.float32).astype(jnp.bfloat16)

def window_mask(query_start, key_start, rows, key_count, back, ahead, frames, block):
    query_pos = query_start + jnp.arange(rows, dtype=jnp.int32)
    key_pos = key_start + jnp.arange(key_count, dtype=jnp.int32)
    query_block = query_pos // block
    key_block = key_pos // block
    back_rows = jnp.repeat(back, block, total_repeat_length=rows)
    ahead_rows = jnp.repeat(ahead, block, total_repeat_length=rows)
    lower = (query_block - back_rows)[:, None]
    upper = (query_block + ahead_rows)[:, None]
    inside = (key_pos >= 0) & (key_pos < frames)
    return (key_block[None, :] >= lower) & (key_block[None, :] <= upper) & inside[None, :]

def window_attention(query, keys, values, allowed, heads):
    rows, width = query.shape
    size = width // heads
    query_heads = query.reshape(rows, heads, size).transpose(1, 0, 2)
    key_heads = keys.reshape(-1, heads, size).transpose(1, 0, 2)
    value_heads = values.reshape(-1, heads, size).transpose(1, 0, 2)

    def one_head(operands):
        query_one, key_one, value_one = operands
        scores = jnp.dot(query_one, key_one.T, preferred_element_type=jnp.float32) / math.sqrt(size)
        scores = jnp.where(allowed, scores, -1e+30)
        top = lax.optimization_barrier(jnp.max(scores, axis=-1, keepdims=True))
        weights = jnp.exp(scores - top)
        total = lax.optimization_barrier(jnp.sum(weights, axis=-1, keepdims=True))
        probs = (weights / total).astype(jnp.bfloat16)
        return jnp.dot(probs, value_one, preferred_element_type=jnp.float32).astype(jnp.bfloat16)
    context = lax.map(one_head, (query_heads, key_heads, value_heads))
    return context.transpose(1, 0, 2).reshape(rows, width)

def branch_velocity(rows, proj_weight):
    normed = layer_norm(rows.astype(jnp.float32)).astype(jnp.bfloat16)
    return lax.dot_general(proj_weight, normed, (((0,), (1,)), ((), ())), preferred_element_type=jnp.float32)

def reference(hidden, latent, prompt_mel, window_back, window_ahead, step_index, proj_weight, latent_weight, prompt_weight, time_weight, qkv_weight, attn_out_weight):
    spans = FRAMES // FR
    per_span = FR // BLK
    grouped = hidden.reshape(spans, 2, FR, D)

    def span_velocity(pair):
        return (branch_velocity(pair[0], proj_weight), branch_velocity(pair[1], proj_weight))
    cond_vel, free_vel = lax.map(span_velocity, grouped)
    cond_vel = cond_vel.transpose(1, 0, 2).reshape(MEL, FRAMES)
    free_vel = free_vel.transpose(1, 0, 2).reshape(MEL, FRAMES)
    delta = time_value(step_index[0] + 1) - time_value(step_index[0])
    latent_next = latent + delta * (cond_vel + GUIDE * (cond_vel - free_vel))
    shift, scale, gate = modulation(step_index, time_weight)
    padded_latent = jnp.pad(latent_next, ((0, 0), (HALO, HALO)))
    padded_prompt = jnp.pad(prompt_mel, ((0, 0), (HALO, HALO)))

    def span_layer(index):
        start = (index * FR).astype(jnp.int32)
        latent_win = lax.dynamic_slice_in_dim(padded_latent, start, FR + 2 * HALO, 1)
        prompt_win = lax.dynamic_slice_in_dim(padded_prompt, start, FR + 2 * HALO, 1)
        back = lax.dynamic_slice_in_dim(window_back, (index * per_span).astype(jnp.int32), per_span, 0)
        ahead = lax.dynamic_slice_in_dim(window_ahead, (index * per_span).astype(jnp.int32), per_span, 0)
        allowed = window_mask(start, start - HALO, FR, FR + 2 * HALO, back, ahead, FRAMES, BLK)
        results = []
        for flag in (1.0, 0.0):
            first = embed_rows(latent_win, prompt_win, jnp.float32(flag), latent_weight, prompt_weight)
            packed = attention_input(first, shift, scale, qkv_weight)
            context = window_attention(packed[HALO:HALO + FR, :D], packed[:, D:2 * D], packed[:, 2 * D:], allowed, HEADS)
            projected = jnp.dot(context, attn_out_weight, preferred_element_type=jnp.float32)
            results.append((first[HALO:HALO + FR] + gate * projected).astype(jnp.bfloat16))
        return jnp.stack(results)
    layered = lax.map(span_layer, jnp.arange(spans, dtype=jnp.int32))
    return (latent_next, layered.reshape(2 * FRAMES, D))
```

```python
import functools
import math

import jax
import jax.numpy as jnp
from jax import lax
from jax.experimental import pallas as pl
from jax.experimental.pallas import tpu as pltpu
from jax.sharding import PartitionSpec as P

HEADS = 16
BLK = 32
NSTEPS = 32
HALO = 128
EPS = 1e-06
GUIDE = 0.5
TILE = 128
MASKED = -1e30
SMALL = 1e-30
LARGE = 1e30

F32 = jnp.float32
BF16 = jnp.bfloat16
VMEM_LIMIT = 48 * 1024 * 1024


def mm(a, b):
    return jnp.dot(a, b, preferred_element_type=F32)


def mm_nt(a, b):
    return lax.dot_general(a, b, (((1,), (1,)), ((), ())), preferred_element_type=F32)


def whole(memory_space=pltpu.VMEM):
    return pl.BlockSpec(memory_space=memory_space)


def time_value(step):
    return 1.0 - jnp.cos(0.5 * math.pi * step.astype(F32) / NSTEPS)


def time_features(step_index, freq):
    later = time_value(step_index[0] + 1)
    half_freq = freq // 2
    freqs = jnp.exp(-math.log(10000.0) * jnp.arange(half_freq, dtype=F32) / half_freq)
    angles = 1000.0 * later * freqs
    return jnp.concatenate([jnp.sin(angles), jnp.cos(angles)])[None, :]


def velocity_kernel(hidden_ref, weight_ref, vel_ref, sent_ref):
    rows = hidden_ref[...].astype(F32)
    mean = jnp.mean(rows, axis=-1, keepdims=True)
    centered = rows - mean
    spread = jnp.mean(centered * centered, axis=-1, keepdims=True)
    normed = (centered * lax.rsqrt(spread + EPS)).astype(BF16)
    vel = mm(normed, weight_ref[...]).T
    vel_ref[...] = vel
    sent_ref[...] = vel.astype(BF16)


def velocity_call(hidden, proj_weight):
    rows, width = hidden.shape
    mel = proj_weight.shape[1]
    step = 128
    return pl.pallas_call(
        velocity_kernel,
        grid=(rows // step,),
        in_specs=[
            pl.BlockSpec((step, width), lambda i: (i, 0)),
            pl.BlockSpec((width, mel), lambda i: (0, 0)),
        ],
        out_specs=[
            pl.BlockSpec((mel, step), lambda i: (0, i)),
            pl.BlockSpec((mel, step), lambda i: (0, i)),
        ],
        out_shape=[
            jax.ShapeDtypeStruct((mel, rows), F32),
            jax.ShapeDtypeStruct((mel, rows), BF16),
        ],
        cost_estimate=pl.CostEstimate(
            flops=2 * rows * width * mel, bytes_accessed=2 * rows * width, transcendentals=0
        ),
        name="velocity",
    )(hidden, proj_weight)


def prepare_kernel(
    ints_ref,
    back_ref,
    ahead_ref,
    feats_ref,
    latent_w_ref,
    prompt_w_ref,
    time_w_ref,
    qkv_ref,
    mixed_ref,
    keyed_ref,
    gram_ref,
    embed_ref,
    gate_ref,
    bias_ref,
    left_ref,
):
    step = pl.program_id(0)
    mel, width = latent_w_ref.shape

    @pl.when(step == 0)
    def _():
        feats = feats_ref[...]
        high = feats.astype(BF16)
        rest = feats - high.astype(F32)
        mid = rest.astype(BF16)
        low = (rest - mid.astype(F32)).astype(BF16)
        stacked = jnp.concatenate([high, mid, low], axis=0)
        parts = mm(stacked, time_w_ref[...])
        freq_rows = high.shape[0]
        mod = parts[0:1] + (
            parts[freq_rows : freq_rows + 1] + parts[2 * freq_rows : 2 * freq_rows + 1]
        )
        shift, scale, gate = mod[:, :width], mod[:, width : 2 * width], mod[:, 2 * width :]
        gate_ref[...] = gate
        both = jnp.concatenate([latent_w_ref[...], prompt_w_ref[...]], axis=0)
        embed = jnp.concatenate(
            [both, latent_w_ref[...], jnp.zeros((256 - 3 * mel, width), BF16)], axis=0
        )
        embed_ref[...] = embed
        wide = both.astype(F32)
        centered = wide - jnp.mean(wide, axis=-1, keepdims=True)
        left_ref[0 : 2 * mel] = (centered * (1.0 + scale)).astype(BF16)
        shift_high = shift.astype(BF16).astype(F32)
        which = lax.broadcasted_iota(jnp.int32, (16, width), 0)
        left_ref[2 * mel : 2 * mel + 16] = jnp.where(
            which == 0, shift_high, jnp.where(which == 1, shift - shift_high, 0.0)
        ).astype(BF16)
        col = jnp.mean(embed.astype(F32), axis=-1, keepdims=True)
        row = mm_nt(jnp.ones((16, width), BF16), embed)[0:1] / width
        gram = mm_nt(embed, embed) / width - col * row
        gram_high = gram.astype(BF16)
        gram_ref[0:256] = gram_high
        gram_ref[256:512] = (gram - gram_high.astype(F32)).astype(BF16)
        half = ints_ref[0]
        first_block = ints_ref[2]
        total_blocks = ints_ref[3]
        per_half = back_ref.shape[0] // 2
        keys = bias_ref.shape[1]
        row_block = lax.broadcasted_iota(jnp.int32, (16, keys), 0)
        lower = jnp.zeros((16, keys), jnp.int32)
        upper = jnp.zeros((16, keys), jnp.int32)
        for block in range(per_half):
            lower = jnp.where(row_block == block, block - back_ref[half * per_half + block], lower)
            upper = jnp.where(row_block == block, block + ahead_ref[half * per_half + block], upper)
        key_block = lax.broadcasted_iota(jnp.int32, (16, keys), 1) // BLK - HALO // BLK
        place = key_block + first_block
        seen = (key_block >= lower) & (key_block <= upper) & (place >= 0) & (place < total_blocks)
        bias_ref[0:16] = jnp.where(seen, 0.0, MASKED).astype(BF16)
        bias_ref[16:128] = jnp.zeros((112, keys), BF16)

    acc = mm(left_ref[...], qkv_ref[...])
    columns = acc.shape[1]
    acc = acc * jnp.where(step < 2, math.log2(math.e) / math.sqrt(width // HEADS), 1.0)
    offset = acc[2 * mel : 2 * mel + 1] + acc[2 * mel + 1 : 2 * mel + 2]
    offset_high = offset.astype(BF16).astype(F32)
    which = lax.broadcasted_iota(jnp.int32, (256 - 3 * mel, columns), 0)
    last = jnp.where(which == 0, offset_high, jnp.where(which == 1, offset - offset_high, 0.0))
    block = jnp.concatenate([acc[: 2 * mel], acc[:mel], last], axis=0)
    mixed_ref[...] = block.astype(BF16)

    @pl.when((step == 2) | (step == 3))
    def _():
        keyed_ref[...] = block.T.astype(BF16)


def prepare_call(ints, back, ahead, feats, latent_weight, prompt_weight, time_weight, qkv_weight):
    mel, width = latent_weight.shape
    step = 512
    steps = 3 * width // step
    fixed = lambda j: (0, 0)
    smem = pl.BlockSpec(memory_space=pltpu.SMEM)
    return pl.pallas_call(
        prepare_kernel,
        grid=(steps,),
        in_specs=[
            smem,
            smem,
            smem,
            pl.BlockSpec(feats.shape, fixed),
            pl.BlockSpec((mel, width), fixed),
            pl.BlockSpec((mel, width), fixed),
            pl.BlockSpec(time_weight.shape, fixed),
            pl.BlockSpec((width, step), lambda j: (0, j)),
        ],
        out_specs=[
            pl.BlockSpec((256, step), lambda j: (0, j)),
            pl.BlockSpec((step, 256), lambda j: (jnp.clip(j - 2, 0, 1), 0)),
            pl.BlockSpec((512, 256), fixed),
            pl.BlockSpec((256, width), fixed),
            pl.BlockSpec((1, width), fixed),
            pl.BlockSpec((128, 512 + 2 * HALO), fixed),
        ],
        out_shape=[
            jax.ShapeDtypeStruct((256, 3 * width), BF16),
            jax.ShapeDtypeStruct((width, 256), BF16),
            jax.ShapeDtypeStruct((512, 256), BF16),
            jax.ShapeDtypeStruct((256, width), BF16),
            jax.ShapeDtypeStruct((1, width), F32),
            jax.ShapeDtypeStruct((128, 512 + 2 * HALO), BF16),
        ],
        scratch_shapes=[pltpu.VMEM((2 * mel + 16, width), BF16)],
        compiler_params=pltpu.CompilerParams(vmem_limit_bytes=VMEM_LIMIT),
        cost_estimate=pl.CostEstimate(
            flops=2 * 256 * width * 3 * width, bytes_accessed=8 * width * width, transcendentals=0
        ),
        name="prepare",
    )(ints, back, ahead, feats, latent_weight, prompt_weight, time_weight, qkv_weight)


def combine_kernel(
    ints_ref,
    floats_ref,
    vel_ref,
    partner_ref,
    latent_ref,
    prompt_ref,
    next_ref,
    rows_ref,
    seq_ref,
    cross_ref,
):
    half, branch = ints_ref[0], ints_ref[1]
    mel, frames = vel_ref.shape
    updated = latent_ref[...] + (
        floats_ref[0] * vel_ref[...] + floats_ref[1] * partner_ref[...].astype(F32)
    )
    share = frames // 2
    next_ref[...] = jnp.where(branch == 0, updated[:, :share], updated[:, share:])
    high = updated.astype(BF16)
    rows_ref[0:mel] = high
    prompt = prompt_ref[...]
    rows_ref[mel : 2 * mel] = (prompt * floats_ref[2]).astype(BF16)
    rows_ref[2 * mel : 3 * mel] = (updated - high.astype(F32)).astype(BF16)
    rows_ref[3 * mel : 256] = jnp.zeros((256 - 3 * mel, frames), BF16)
    head, tail = updated[:, :HALO], updated[:, frames - HALO :]
    seq_ref[0:mel] = jnp.where(half == 0, head, tail).astype(BF16)
    seq_ref[mel : 2 * mel] = jnp.where(
        half == 0, prompt[:, :HALO], prompt[:, frames - HALO :]
    ).astype(BF16)
    cross_ref[...] = jnp.where(half == 0, tail, head).astype(BF16)


def combine_call(ints, floats, vel, partner, latent, prompt):
    mel, frames = vel.shape
    fixed = lambda i, ints: (0, 0)
    mine = lambda i, ints: (0, ints[0])
    return pl.pallas_call(
        combine_kernel,
        grid_spec=pltpu.PrefetchScalarGridSpec(
            num_scalar_prefetch=1,
            grid=(1,),
            in_specs=[
                pl.BlockSpec(memory_space=pltpu.SMEM),
                pl.BlockSpec((mel, frames), fixed),
                pl.BlockSpec((mel, frames), fixed),
                pl.BlockSpec((mel, frames), mine),
                pl.BlockSpec((mel, frames), mine),
            ],
            out_specs=[
                pl.BlockSpec((mel, frames // 2), fixed),
                pl.BlockSpec((256, frames), fixed),
                pl.BlockSpec((2 * mel, HALO), fixed),
                pl.BlockSpec((mel, HALO), fixed),
            ],
        ),
        out_shape=[
            jax.ShapeDtypeStruct((mel, frames // 2), F32),
            jax.ShapeDtypeStruct((256, frames), BF16),
            jax.ShapeDtypeStruct((2 * mel, HALO), BF16),
            jax.ShapeDtypeStruct((mel, HALO), BF16),
        ],
        name="combine",
    )(ints, floats, vel, partner, latent, prompt)


def layer_kernel(
    ints_ref,
    floats_ref,
    own_ref,
    seq_ref,
    cross_ref,
    prompt_ref,
    mixed_ref,
    keyed_ref,
    gram_ref,
    embed_ref,
    bias_ref,
    gate_ref,
    out_w_ref,
    next_ref,
    query_ref,
    key_ref,
    value_ref,
    context_ref,
):
    half = ints_ref[0]
    flag = floats_ref[2]
    mel = cross_ref.shape[0]
    frames = own_ref.shape[1]
    width = embed_ref.shape[1]
    keys = frames + 2 * HALO
    pairs = width // 128
    own = own_ref[...]
    blank = jnp.zeros((256 - 2 * mel, HALO), F32)
    seq_rows = jnp.concatenate(
        [seq_ref[0:mel].astype(F32), seq_ref[mel : 2 * mel].astype(F32) * flag, blank], axis=0
    )
    cross_rows = jnp.concatenate(
        [cross_ref[...].astype(F32), prompt_ref[...] * flag, blank], axis=0
    )
    before = jnp.where(half == 0, seq_rows, cross_rows).astype(BF16)
    after = jnp.where(half == 0, cross_rows, seq_rows).astype(BF16)
    rows = jnp.concatenate([before, own, after], axis=1)
    weighted = mm(gram_ref[0:256], rows) + mm(gram_ref[256:512], rows)
    rows = rows.astype(F32)
    spread = jnp.sum(weighted * rows, axis=0, keepdims=True)
    inverse = lax.rsqrt(jnp.maximum(spread, 0.0) + EPS)
    latent = (rows[0:mel] + rows[2 * mel : 3 * mel]) * inverse
    high = latent.astype(BF16)
    which = lax.broadcasted_iota(jnp.int32, (256 - 3 * mel, keys), 0)
    normed = jnp.concatenate(
        [
            high,
            (rows[mel : 2 * mel] * inverse).astype(BF16),
            (latent - high.astype(F32)).astype(BF16),
            jnp.where(which < 2, 1.0, 0.0).astype(BF16),
        ],
        axis=0,
    )
    turned = normed.T
    for start in range(0, width, 256):
        cols = slice(start, start + 256)
        key_ref[cols] = mm(keyed_ref[cols], normed).astype(BF16)
        value_ref[:, cols] = mm(turned, mixed_ref[:, 2 * width + start : 2 * width + start + 256]).astype(BF16)
        query_ref[:, cols] = mm(turned[HALO : HALO + frames], mixed_ref[:, cols]).astype(BF16)

    lane = lax.broadcasted_iota(jnp.int32, (TILE, 128), 1)
    row = lax.broadcasted_iota(jnp.int32, (TILE, 128), 0)
    left = lane < 64
    ones = jnp.ones((TILE + 2 * HALO, 128), BF16)

    def attend(tile, pair, stable):
        at = tile * TILE
        cols = pl.ds(pair * 128, 128)
        window = pl.ds(at, TILE + 2 * HALO)
        query = query_ref[pl.ds(at, TILE), cols]
        zero = jnp.zeros_like(query)
        chosen = (lane == tile * (TILE // BLK) + row // BLK).astype(F32).astype(BF16)
        stacked = jnp.concatenate(
            [
                jnp.concatenate([jnp.where(left, query, zero), chosen], axis=1),
                jnp.concatenate([jnp.where(left, zero, query), chosen], axis=1),
            ],
            axis=0,
        )
        right = jnp.concatenate([key_ref[cols, window], bias_ref[:, window]], axis=0)
        scores = mm(stacked, right)
        if stable:
            scores = scores - jnp.max(scores, axis=-1, keepdims=True)
        probs = jnp.exp2(scores).astype(BF16)
        values = jnp.concatenate([value_ref[window, cols], ones], axis=1)
        both = mm(probs, values)
        total = jnp.where(left, both[:TILE, 128:], both[TILE:, 128:])
        context = jnp.where(left, both[:TILE, :128], both[TILE:, :128]) / total
        context_ref[pl.ds(at, TILE), cols] = context.astype(BF16)
        return total

    least = jnp.full((TILE, 128), 1.0, F32)
    most = jnp.full((TILE, 128), 1.0, F32)
    for tile in range(frames // TILE):
        for pair in range(pairs):
            total = attend(tile, pair, False)
            least = jnp.minimum(least, total)
            most = jnp.maximum(most, total)
    safe = (jnp.min(least) > SMALL) & (jnp.max(most) < LARGE)

    @pl.when(jnp.logical_not(safe))
    def _():
        def one(index, carry):
            attend(index // pairs, index % pairs, True)
            return carry

        lax.fori_loop(0, frames // TILE * pairs, one, 0)

    own_turned = own.T
    gate = gate_ref[...]
    for start in range(0, width, 256):
        cols = slice(start, start + 256)
        first = mm(own_turned, embed_ref[:, cols])
        projected = mm(context_ref[...], out_w_ref[:, cols])
        next_ref[:, cols] = (first + gate[:, cols] * projected).astype(BF16)


def layer_call(ints, floats, own, seq, cross, prompt, mixed, keyed, gram, embed, bias, gate, out_w):
    mel = cross.shape[0]
    frames = own.shape[1]
    width = embed.shape[1]
    keys = frames + 2 * HALO
    fixed = lambda i, ints: (0, 0)
    blocks = frames // HALO

    def full(array):
        return pl.BlockSpec(array.shape, fixed)

    return pl.pallas_call(
        layer_kernel,
        grid_spec=pltpu.PrefetchScalarGridSpec(
            num_scalar_prefetch=1,
            grid=(1,),
            in_specs=[
                pl.BlockSpec(memory_space=pltpu.SMEM),
                full(own),
                full(seq),
                full(cross),
                pl.BlockSpec((mel, HALO), lambda i, ints: (0, blocks - ints[0])),
                full(mixed),
                full(keyed),
                full(gram),
                full(embed),
                full(bias),
                full(gate),
                full(out_w),
            ],
            out_specs=pl.BlockSpec((frames, width), fixed),
            scratch_shapes=[
                pltpu.VMEM((frames, width), BF16),
                pltpu.VMEM((width, keys), BF16),
                pltpu.VMEM((keys, width), BF16),
                pltpu.VMEM((frames, width), BF16),
            ],
        ),
        out_shape=jax.ShapeDtypeStruct((frames, width), BF16),
        compiler_params=pltpu.CompilerParams(vmem_limit_bytes=VMEM_LIMIT),
        cost_estimate=pl.CostEstimate(
            flops=4_000_000_000, bytes_accessed=6_000_000, transcendentals=3_000_000
        ),
        name="layer",
    )(ints, floats, own, seq, cross, prompt, mixed, keyed, gram, embed, bias, gate, out_w)


def body(
    hidden,
    latent,
    prompt_mel,
    window_back,
    window_ahead,
    step_index,
    proj_weight,
    latent_weight,
    prompt_weight,
    time_weight,
    qkv_weight,
    attn_out_weight,
):
    axes = ("seq", "cfg")
    spans = lax.axis_size("seq")
    rows, width = hidden.shape
    place = lax.axis_index("cfg")
    branch, half = place % 2, place // 2
    first_block = (2 * lax.axis_index("seq") + half) * (rows // BLK)
    total_blocks = 2 * spans * (rows // BLK)
    ints = jnp.stack([half, branch, first_block, jnp.int32(total_blocks)]).astype(jnp.int32)
    delta = time_value(step_index[0] + 1) - time_value(step_index[0])
    mine = jnp.where(branch == 0, 1.0 + GUIDE, -GUIDE)
    other = jnp.where(branch == 0, -GUIDE, 1.0 + GUIDE)
    flag = jnp.where(branch == 0, 1.0, 0.0)
    floats = jnp.stack([delta * mine, delta * other, flag]).astype(F32)

    def at(span, cell):
        return span * 4 + cell

    everyone = [(span, cell) for span in range(spans) for cell in range(4)]
    to_partner = [(at(s, c), at(s, c ^ 1)) for s, c in everyone]
    to_half = [(at(s, c), at(s, c ^ 3)) for s, c in everyone]
    to_seq = [
        (at(s, c), at(s + (1 if c >= 2 else -1), c ^ 3))
        for s, c in everyone
        if 0 <= s + (1 if c >= 2 else -1) < spans
    ]
    vel, sent = velocity_call(hidden, proj_weight)
    partner = lax.ppermute(sent, axes, to_partner)
    feats = jnp.broadcast_to(time_features(step_index, time_weight.shape[0]), (16, time_weight.shape[0]))
    mixed, keyed, gram, embed, gate, bias = prepare_call(
        ints, window_back, window_ahead, feats, latent_weight, prompt_weight, time_weight, qkv_weight
    )
    latent_out, own, seq, cross = combine_call(ints, floats, vel, partner, latent, prompt_mel)
    cross = lax.ppermute(cross, axes, to_half)
    seq = lax.ppermute(seq, axes, to_seq)
    hidden_next = layer_call(
        ints, floats, own, seq, cross, prompt_mel, mixed, keyed, gram, embed, bias, gate, attn_out_weight
    )
    return (latent_out, hidden_next)


def solution(mesh):
    in_specs = (
        P(("seq", "cfg"), None),
        P(None, "seq"),
        P(None, "seq"),
        P("seq"),
        P("seq"),
        P(),
        P(),
        P(),
        P(),
        P(),
        P(),
        P(),
    )
    out_specs = (P(None, ("seq", "cfg")), P(("seq", "cfg"), None))
    return jax.shard_map(body, mesh=mesh, in_specs=in_specs, out_specs=out_specs, check_vma=False)
```

```python
import functools
import math

import jax
import jax.numpy as jnp
from jax import lax
from jax.experimental import pallas as pl
from jax.experimental.pallas import tpu as pltpu
from jax.sharding import PartitionSpec as P

HEADS = 16
BLK = 32
NSTEPS = 32
HALO = 128
EPS = 1e-06
GUIDE = 0.5
TILE = 128
MASKED = -1e30
SMALL = 1e-30
LARGE = 1e30

F32 = jnp.float32
BF16 = jnp.bfloat16
VMEM_LIMIT = 24 * 1024 * 1024
SMALL_VMEM = 8 * 1024 * 1024


def mm(a, b):
    return jnp.dot(a, b, preferred_element_type=F32)


def mm_nt(a, b):
    return lax.dot_general(a, b, (((1,), (1,)), ((), ())), preferred_element_type=F32)


def whole(memory_space=pltpu.VMEM):
    return pl.BlockSpec(memory_space=memory_space)


def in_hbm(array):
    return pltpu.with_memory_space_constraint(array, pltpu.HBM)


def location():
    place = lax.axis_index("cfg")
    half = place // 2
    return half, place % 2, 2 * lax.axis_index("seq") + half


def time_value(step):
    return 1.0 - jnp.cos(0.5 * math.pi * step.astype(F32) / NSTEPS)


def time_features(step_index, freq):
    later = time_value(step_index[0] + 1)
    half_freq = freq // 2
    freqs = jnp.exp(-math.log(10000.0) * jnp.arange(half_freq, dtype=F32) / half_freq)
    angles = 1000.0 * later * freqs
    return jnp.concatenate([jnp.sin(angles), jnp.cos(angles)])[None, :]


def velocity_kernel(hidden_ref, weight_ref, vel_ref, sent_ref, rows_ref, held_ref, sems):
    parts = sems.shape[0] - 1
    step = hidden_ref.shape[0] // parts
    copies = [pltpu.make_async_copy(weight_ref, held_ref, sems.at[parts])]
    for part in range(parts):
        here = pl.ds(part * step, step)
        copies.append(
            pltpu.make_async_copy(hidden_ref.at[here], rows_ref.at[here], sems.at[part])
        )
    for copy in copies:
        copy.start()
    copies[0].wait()
    weight = held_ref[...]
    for part in range(parts):
        copies[part + 1].wait()
        here = slice(part * step, (part + 1) * step)
        rows = rows_ref[here].astype(F32)
        mean = jnp.mean(rows, axis=-1, keepdims=True)
        centered = rows - mean
        spread = jnp.mean(centered * centered, axis=-1, keepdims=True)
        normed = (centered * lax.rsqrt(spread + EPS)).astype(BF16)
        vel = mm_nt(weight, normed)
        vel_ref[:, here] = vel
        sent_ref[:, here] = vel.astype(BF16)


def velocity_call(hidden, proj_turned):
    rows, width = hidden.shape
    mel = proj_turned.shape[0]
    return pl.pallas_call(
        velocity_kernel,
        in_specs=[whole(pltpu.HBM)] * 2,
        out_specs=[whole(), whole()],
        out_shape=[
            jax.ShapeDtypeStruct((mel, rows), F32),
            jax.ShapeDtypeStruct((mel, rows), BF16),
        ],
        scratch_shapes=[
            pltpu.VMEM((rows, width), BF16),
            pltpu.VMEM((mel, width), BF16),
            pltpu.SemaphoreType.DMA((5,)),
        ],
        compiler_params=pltpu.CompilerParams(vmem_limit_bytes=SMALL_VMEM),
        cost_estimate=pl.CostEstimate(
            flops=2 * rows * width * mel, bytes_accessed=2 * rows * width, transcendentals=0
        ),
        name="velocity",
    )(in_hbm(hidden), in_hbm(proj_turned))


def prepare_kernel(
    total_blocks,
    feats_ref,
    back_hbm,
    ahead_hbm,
    latent_w_hbm,
    prompt_w_hbm,
    time_w_hbm,
    qkv_hbm,
    mixed_ref,
    keyed_ref,
    gram_ref,
    embed_ref,
    gate_ref,
    bias_ref,
    left_ref,
    back_ref,
    ahead_ref,
    latent_w_ref,
    prompt_w_ref,
    time_w_ref,
    qkv_ref,
    sems,
):
    mel, width = latent_w_ref.shape
    small = [
        pltpu.make_async_copy(source, target, sems.at[index])
        for index, (source, target) in enumerate(
            [
                (latent_w_hbm, latent_w_ref),
                (prompt_w_hbm, prompt_w_ref),
                (time_w_hbm, time_w_ref),
                (back_hbm, back_ref),
                (ahead_hbm, ahead_ref),
            ]
        )
    ]
    parts = 6
    columns = 3 * width // parts
    large = []
    for part in range(parts):
        here = pl.ds(part * columns, columns)
        large.append(
            pltpu.make_async_copy(qkv_hbm.at[:, here], qkv_ref.at[:, here], sems.at[5 + part])
        )
    for copy in small + large:
        copy.start()

    small[0].wait()
    small[1].wait()
    both = jnp.concatenate([latent_w_ref[...], prompt_w_ref[...]], axis=0)
    wide = both.astype(F32)
    centered = wide - jnp.mean(wide, axis=-1, keepdims=True)
    embed = jnp.concatenate(
        [both, latent_w_ref[...], jnp.zeros((256 - 3 * mel, width), BF16)], axis=0
    )
    embed_ref[...] = embed
    col = jnp.mean(embed.astype(F32), axis=-1, keepdims=True)
    row = mm_nt(jnp.ones((16, width), BF16), embed)[0:1] / width
    gram = mm_nt(embed, embed) / width - col * row
    gram_high = gram.astype(BF16)
    gram_ref[0:256] = gram_high
    gram_ref[256:512] = (gram - gram_high.astype(F32)).astype(BF16)

    feats = jnp.broadcast_to(feats_ref[...], (16, feats_ref.shape[1]))
    high = feats.astype(BF16)
    rest = feats - high.astype(F32)
    mid = rest.astype(BF16)
    low = (rest - mid.astype(F32)).astype(BF16)
    small[2].wait()
    pieces = mm(jnp.concatenate([high, mid, low], axis=0), time_w_ref[...])
    mod = pieces[0:1] + (pieces[16:17] + pieces[32:33])
    shift, scale, gate = mod[:, :width], mod[:, width : 2 * width], mod[:, 2 * width :]
    gate_ref[...] = gate
    left_ref[0 : 2 * mel] = (centered * (1.0 + scale)).astype(BF16)
    shift_high = shift.astype(BF16).astype(F32)
    which = lax.broadcasted_iota(jnp.int32, (16, width), 0)
    left_ref[2 * mel : 2 * mel + 16] = jnp.where(
        which == 0, shift_high, jnp.where(which == 1, shift - shift_high, 0.0)
    ).astype(BF16)

    small[3].wait()
    small[4].wait()
    half, _, span = location()
    per_half = back_ref.shape[0] // 2
    keys = bias_ref.shape[1]
    row_block = lax.broadcasted_iota(jnp.int32, (16, keys), 0)
    lower = jnp.zeros((16, keys), jnp.int32)
    upper = jnp.zeros((16, keys), jnp.int32)
    for block in range(per_half):
        lower = jnp.where(row_block == block, block - back_ref[half * per_half + block], lower)
        upper = jnp.where(row_block == block, block + ahead_ref[half * per_half + block], upper)
    key_block = lax.broadcasted_iota(jnp.int32, (16, keys), 1) // BLK - HALO // BLK
    place = key_block + span * per_half
    seen = (key_block >= lower) & (key_block <= upper) & (place >= 0) & (place < total_blocks)
    bias_ref[0:16] = jnp.where(seen, 0.0, MASKED).astype(BF16)
    bias_ref[16:128] = jnp.zeros((112, keys), BF16)

    left = left_ref[...]
    for part, copy in enumerate(large):
        start = part * columns
        copy.wait()
        acc = mm(left, qkv_ref[:, start : start + columns])
        if start < width:
            acc = acc * (math.log2(math.e) / math.sqrt(width // HEADS))
        offset = acc[2 * mel : 2 * mel + 1] + acc[2 * mel + 1 : 2 * mel + 2]
        offset_high = offset.astype(BF16).astype(F32)
        which = lax.broadcasted_iota(jnp.int32, (256 - 3 * mel, columns), 0)
        last = jnp.where(which == 0, offset_high, jnp.where(which == 1, offset - offset_high, 0.0))
        block = jnp.concatenate([acc[: 2 * mel], acc[:mel], last], axis=0).astype(BF16)
        if start < width:
            mixed_ref[:, start : start + columns] = block
        elif start < 2 * width:
            keyed_ref[start - width : start - width + columns] = block.T
        else:
            mixed_ref[:, start - width : start - width + columns] = block


def prepare_call(
    total_blocks, back, ahead, feats, latent_weight, prompt_weight, time_weight, qkv_weight
):
    mel, width = latent_weight.shape
    return pl.pallas_call(
        functools.partial(prepare_kernel, total_blocks),
        in_specs=[whole()] + [whole(pltpu.HBM)] * 6,
        out_specs=[whole()] * 6,
        out_shape=[
            jax.ShapeDtypeStruct((256, 2 * width), BF16),
            jax.ShapeDtypeStruct((width, 256), BF16),
            jax.ShapeDtypeStruct((512, 256), BF16),
            jax.ShapeDtypeStruct((256, width), BF16),
            jax.ShapeDtypeStruct((1, width), F32),
            jax.ShapeDtypeStruct((128, 512 + 2 * HALO), BF16),
        ],
        scratch_shapes=[
            pltpu.VMEM((2 * mel + 16, width), BF16),
            pltpu.SMEM(back.shape, jnp.int32),
            pltpu.SMEM(ahead.shape, jnp.int32),
            pltpu.VMEM(latent_weight.shape, BF16),
            pltpu.VMEM(prompt_weight.shape, BF16),
            pltpu.VMEM(time_weight.shape, BF16),
            pltpu.VMEM(qkv_weight.shape, BF16),
            pltpu.SemaphoreType.DMA((11,)),
        ],
        compiler_params=pltpu.CompilerParams(vmem_limit_bytes=VMEM_LIMIT),
        cost_estimate=pl.CostEstimate(
            flops=2 * 256 * width * 3 * width, bytes_accessed=8 * width * width, transcendentals=0
        ),
        name="prepare",
    )(
        feats,
        in_hbm(back),
        in_hbm(ahead),
        in_hbm(latent_weight),
        in_hbm(prompt_weight),
        in_hbm(time_weight),
        in_hbm(qkv_weight),
    )


def combine_kernel(
    delta_ref,
    vel_ref,
    partner_ref,
    latent_ref,
    prompt_ref,
    next_ref,
    rows_ref,
    seq_ref,
    cross_ref,
):
    half, branch, _ = location()
    mel, frames = vel_ref.shape
    delta = delta_ref[0]
    mine = jnp.where(branch == 0, 1.0 + GUIDE, -GUIDE) * delta
    other = jnp.where(branch == 0, -GUIDE, 1.0 + GUIDE) * delta
    latent = jnp.where(half == 0, latent_ref[:, :frames], latent_ref[:, frames:])
    prompt = jnp.where(half == 0, prompt_ref[:, :frames], prompt_ref[:, frames:])
    updated = latent + (mine * vel_ref[...] + other * partner_ref[...].astype(F32))
    head, tail = updated[:, :HALO], updated[:, frames - HALO :]
    seq_ref[0:mel] = jnp.where(half == 0, head, tail).astype(BF16)
    seq_ref[mel : 2 * mel] = jnp.where(
        half == 0, prompt[:, :HALO], prompt[:, frames - HALO :]
    ).astype(BF16)
    cross_ref[...] = jnp.where(half == 0, tail, head).astype(BF16)
    share = frames // 2
    next_ref[...] = jnp.where(branch == 0, updated[:, :share], updated[:, share:])
    high = updated.astype(BF16)
    rows_ref[0:mel] = high
    rows_ref[mel : 2 * mel] = jnp.where(branch == 0, prompt, 0.0).astype(BF16)
    rows_ref[2 * mel : 3 * mel] = (updated - high.astype(F32)).astype(BF16)
    rows_ref[3 * mel : 256] = jnp.zeros((256 - 3 * mel, frames), BF16)


def combine_call(delta, vel, partner, latent, prompt):
    mel, frames = vel.shape
    return pl.pallas_call(
        combine_kernel,
        in_specs=[whole(pltpu.SMEM)] + [whole()] * 4,
        out_specs=[whole()] * 4,
        out_shape=[
            jax.ShapeDtypeStruct((mel, frames // 2), F32),
            jax.ShapeDtypeStruct((256, frames), BF16),
            jax.ShapeDtypeStruct((2 * mel, HALO), BF16),
            jax.ShapeDtypeStruct((mel, HALO), BF16),
        ],
        compiler_params=pltpu.CompilerParams(vmem_limit_bytes=SMALL_VMEM),
        name="combine",
    )(delta, vel, partner, latent, prompt)


def normalised(rows, gram_ref, mel):
    weighted = mm(gram_ref[0:256], rows) + mm(gram_ref[256:512], rows)
    rows = rows.astype(F32)
    spread = jnp.sum(weighted * rows, axis=0, keepdims=True)
    inverse = lax.rsqrt(jnp.maximum(spread, 0.0) + EPS)
    latent = (rows[0:mel] + rows[2 * mel : 3 * mel]) * inverse
    high = latent.astype(BF16)
    which = lax.broadcasted_iota(jnp.int32, (256 - 3 * mel, rows.shape[1]), 0)
    return jnp.concatenate(
        [
            high,
            (rows[mel : 2 * mel] * inverse).astype(BF16),
            (latent - high.astype(F32)).astype(BF16),
            jnp.where(which < 2, 1.0, 0.0).astype(BF16),
        ],
        axis=0,
    )


def split_values(values, start, value_ref):
    left = lax.broadcasted_iota(jnp.int32, (values.shape[0], 128), 1) < 64
    for part in range(2):
        pair = values[:, 128 * part : 128 * (part + 1)]
        at = 2 * start + 256 * part
        value_ref[:, at : at + 128] = jnp.where(left, pair, 0.0).astype(BF16)
        value_ref[:, at + 128 : at + 256] = jnp.where(left, 0.0, pair).astype(BF16)


def pair_queries(query, tile):
    row = lax.broadcasted_iota(jnp.int32, (TILE, 128), 0)
    lane = lax.broadcasted_iota(jnp.int32, (TILE, 128), 1)
    chosen = (lane == tile * (TILE // BLK) + row // BLK).astype(F32).astype(BF16)
    return jnp.concatenate([query, chosen], axis=1)


def pair_scores(queries, key_left, key_right, bias):
    gap = jnp.zeros_like(key_left)
    key = jnp.concatenate(
        [
            jnp.concatenate([key_left, gap, bias], axis=0),
            jnp.concatenate([gap, key_right, bias], axis=0),
        ],
        axis=1,
    )
    return mm(queries, key)


def pair_sums(scores, value_left, value_right):
    left = lax.broadcasted_iota(jnp.int32, value_left.shape, 1) < 64
    ones_left = jnp.where(left, 1.0, 0.0).astype(BF16)
    ones_right = jnp.where(left, 0.0, 1.0).astype(BF16)
    value = jnp.concatenate(
        [
            jnp.concatenate([value_left, ones_left], axis=1),
            jnp.concatenate([value_right, ones_right], axis=1),
        ],
        axis=0,
    )
    return mm(jnp.exp2(scores).astype(BF16), value)


def less_top(scores, tops):
    size = scores.shape[1] // 2
    return jnp.concatenate([scores[:, :size] - tops[0], scores[:, size:] - tops[1]], axis=1)


def top_of(scores):
    size = scores.shape[1] // 2
    return (
        jnp.max(scores[:, :size], axis=-1, keepdims=True),
        jnp.max(scores[:, size:], axis=-1, keepdims=True),
    )


def in_range(least, most):
    return (jnp.min(least) > SMALL) & (jnp.max(most) < LARGE)


def pair_keys(key_ref, pair, window):
    return (
        key_ref[pl.ds(pair * 128, 64), window],
        key_ref[pl.ds(pair * 128 + 64, 64), window],
    )


def pair_values(value_ref, pair, window):
    return (
        value_ref[window, pl.ds(pair * 256, 128)],
        value_ref[window, pl.ds(pair * 256 + 128, 128)],
    )


def inner_kernel(
    mel,
    own_ref,
    mixed_ref,
    keyed_ref,
    gram_ref,
    bias_ref,
    query_ref,
    key_ref,
    value_ref,
    context_ref,
):
    frames, width = query_ref.shape
    pairs = width // 128
    normed = normalised(own_ref[...], gram_ref, mel)
    turned = normed.T
    for start in range(0, width, 256):
        cols = slice(start, start + 256)
        key_ref[cols] = mm(keyed_ref[cols], normed).astype(BF16)
        query_ref[:, cols] = mm(turned, mixed_ref[:, cols]).astype(BF16)
        split_values(
            mm(turned, mixed_ref[:, width + start : width + start + 256]), start, value_ref
        )

    def attend(tile, pair, stable):
        at = tile * TILE
        cols = pl.ds(pair * 128, 128)
        window = pl.ds(at - HALO, TILE + 2 * HALO)
        queries = pair_queries(query_ref[pl.ds(at, TILE), cols], tile)
        scores = pair_scores(
            queries, *pair_keys(key_ref, pair, window), bias_ref[:, pl.ds(at, TILE + 2 * HALO)]
        )
        if stable:
            scores = less_top(scores, top_of(scores))
        sums = pair_sums(scores, *pair_values(value_ref, pair, window))
        total = sums[:, 128:]
        context_ref[pl.ds(at - HALO, TILE), cols] = (sums[:, :128] / total).astype(BF16)
        return total

    first, last = HALO // TILE, (frames - HALO) // TILE
    least = jnp.full((TILE, 128), 1.0, F32)
    most = jnp.full((TILE, 128), 1.0, F32)
    for tile in range(first, last):
        for pair in range(pairs):
            total = attend(tile, pair, False)
            least = jnp.minimum(least, total)
            most = jnp.maximum(most, total)

    @pl.when(jnp.logical_not(in_range(least, most)))
    def _():
        def one(index, carry):
            attend(first + index // pairs, index % pairs, True)
            return carry

        lax.fori_loop(0, (last - first) * pairs, one, 0)


def inner_call(mel, own, mixed, keyed, gram, bias):
    frames = own.shape[1]
    width = keyed.shape[0]
    return pl.pallas_call(
        functools.partial(inner_kernel, mel),
        in_specs=[whole()] * 5,
        out_specs=[whole()] * 4,
        out_shape=[
            jax.ShapeDtypeStruct((frames, width), BF16),
            jax.ShapeDtypeStruct((width, frames), BF16),
            jax.ShapeDtypeStruct((frames, 2 * width), BF16),
            jax.ShapeDtypeStruct((frames - 2 * HALO, width), BF16),
        ],
        compiler_params=pltpu.CompilerParams(vmem_limit_bytes=VMEM_LIMIT),
        cost_estimate=pl.CostEstimate(
            flops=3_000_000_000, bytes_accessed=6_000_000, transcendentals=3_000_000
        ),
        name="inner",
    )(own, mixed, keyed, gram, bias)


def edges_of(frames):
    own = TILE + HALO
    return (
        (0, 0, 0, HALO, 0),
        (frames // TILE - 1, frames - own, HALO, frames + HALO - own, frames + HALO),
    )


def outer_kernel(
    own_ref,
    query_ref,
    key_ref,
    value_ref,
    bias_ref,
    context_ref,
    embed_ref,
    gate_ref,
    out_w_ref,
    done_ref,
    first_ref,
    sums_ref,
    totals_ref,
):
    frames, width = query_ref.shape
    pairs = width // 128
    for edge, (tile, at, _, bias_at, _) in enumerate(edges_of(frames)):
        window = pl.ds(at, TILE + HALO)
        here = slice(edge * TILE, (edge + 1) * TILE)
        for pair in range(pairs):
            cols = slice(pair * 128, (pair + 1) * 128)
            queries = pair_queries(query_ref[tile * TILE : (tile + 1) * TILE, cols], tile)
            scores = pair_scores(
                queries,
                *pair_keys(key_ref, pair, window),
                bias_ref[:, bias_at : bias_at + TILE + HALO],
            )
            sums = pair_sums(scores, *pair_values(value_ref, pair, window))
            sums_ref[here, cols] = sums[:, :128]
            totals_ref[here, cols] = sums[:, 128:]
    own_turned = own_ref[...].T
    for start in range(0, width, 256):
        cols = slice(start, start + 256)
        first = mm(own_turned, embed_ref[:, cols])
        projected = mm(context_ref[...], out_w_ref[:, cols])
        done_ref[:, cols] = (
            first[HALO : frames - HALO] + gate_ref[:, cols] * projected
        ).astype(BF16)
        first_ref[0:HALO, cols] = first[0:HALO]
        first_ref[HALO : 2 * HALO, cols] = first[frames - HALO :]


def outer_call(own, query, key, value, bias, context, embed, gate, out_w):
    frames, width = query.shape
    return pl.pallas_call(
        outer_kernel,
        in_specs=[whole()] * 9,
        out_specs=[whole()] * 4,
        out_shape=[
            jax.ShapeDtypeStruct((frames - 2 * HALO, width), BF16),
            jax.ShapeDtypeStruct((2 * HALO, width), F32),
            jax.ShapeDtypeStruct((2 * TILE, width), F32),
            jax.ShapeDtypeStruct((2 * TILE, width), F32),
        ],
        compiler_params=pltpu.CompilerParams(vmem_limit_bytes=VMEM_LIMIT),
        cost_estimate=pl.CostEstimate(
            flops=3_000_000_000, bytes_accessed=6_000_000, transcendentals=2_000_000
        ),
        name="outer",
    )(own, query, key, value, bias, context, embed, gate, out_w)


def close_kernel(
    near_ref,
    prompt_ref,
    mixed_ref,
    keyed_ref,
    gram_ref,
    bias_ref,
    query_ref,
    key_ref,
    value_ref,
    sums_ref,
    totals_ref,
    first_ref,
    gate_ref,
    out_w_ref,
    done_ref,
    next_ref,
    near_key_ref,
    near_value_ref,
    context_ref,
    edge_ref,
    sems,
):
    half, branch, _ = location()
    frames, width = query_ref.shape
    pairs = width // 128
    mel = near_ref.shape[0] // 3
    inner = pltpu.make_async_copy(done_ref, next_ref.at[pl.ds(HALO, frames - 2 * HALO)], sems.at[0])
    inner.start()
    flag = jnp.where(branch == 0, 1.0, 0.0)
    prompt = jnp.where(
        half == 0, prompt_ref[:, frames : frames + HALO], prompt_ref[:, frames - HALO : frames]
    )
    blank = jnp.zeros((256 - 2 * mel, HALO), F32)
    near = near_ref[...].astype(F32)
    cross_rows = jnp.concatenate([near[0:mel], prompt * flag, blank], axis=0)
    seq_rows = jnp.concatenate(
        [near[mel : 2 * mel], near[2 * mel : 3 * mel] * flag, blank], axis=0
    )
    before = jnp.where(half == 0, seq_rows, cross_rows).astype(BF16)
    after = jnp.where(half == 0, cross_rows, seq_rows).astype(BF16)
    normed = normalised(jnp.concatenate([before, after], axis=1), gram_ref, mel)
    turned = normed.T
    for start in range(0, width, 256):
        cols = slice(start, start + 256)
        near_key_ref[cols] = mm(keyed_ref[cols], normed).astype(BF16)
        split_values(
            mm(turned, mixed_ref[:, width + start : width + start + 256]), start, near_value_ref
        )

    edges = edges_of(frames)
    least = jnp.full((TILE, 128), 1.0, F32)
    most = jnp.full((TILE, 128), 1.0, F32)
    for edge, (tile, _, near_at, _, bias_at) in enumerate(edges):
        window = pl.ds(near_at, HALO)
        here = slice(edge * TILE, (edge + 1) * TILE)
        for pair in range(pairs):
            cols = slice(pair * 128, (pair + 1) * 128)
            queries = pair_queries(query_ref[tile * TILE : (tile + 1) * TILE, cols], tile)
            scores = pair_scores(
                queries,
                *pair_keys(near_key_ref, pair, window),
                bias_ref[:, bias_at : bias_at + HALO],
            )
            sums = pair_sums(scores, *pair_values(near_value_ref, pair, window))
            total = sums[:, 128:] + totals_ref[here, cols]
            context_ref[here, cols] = ((sums[:, :128] + sums_ref[here, cols]) / total).astype(BF16)
            least = jnp.minimum(least, total)
            most = jnp.maximum(most, total)

    @pl.when(jnp.logical_not(in_range(least, most)))
    def _():
        for edge, (tile, at, near_at, bias_own, bias_near) in enumerate(edges):
            here = slice(edge * TILE, (edge + 1) * TILE)

            def one(pair, carry):
                cols = pl.ds(pair * 128, 128)
                own_window = pl.ds(at, TILE + HALO)
                near_window = pl.ds(near_at, HALO)
                queries = pair_queries(query_ref[tile * TILE : (tile + 1) * TILE, cols], tile)
                own_scores = pair_scores(
                    queries,
                    *pair_keys(key_ref, pair, own_window),
                    bias_ref[:, bias_own : bias_own + TILE + HALO],
                )
                near_scores = pair_scores(
                    queries,
                    *pair_keys(near_key_ref, pair, near_window),
                    bias_ref[:, bias_near : bias_near + HALO],
                )
                tops = [
                    jnp.maximum(a, b) for a, b in zip(top_of(own_scores), top_of(near_scores))
                ]
                sums = pair_sums(
                    less_top(own_scores, tops), *pair_values(value_ref, pair, own_window)
                ) + pair_sums(
                    less_top(near_scores, tops), *pair_values(near_value_ref, pair, near_window)
                )
                context_ref[here, cols] = (sums[:, :128] / sums[:, 128:]).astype(BF16)
                return carry

            lax.fori_loop(0, pairs, one, 0)

    for start in range(0, width, 256):
        cols = slice(start, start + 256)
        projected = mm(context_ref[...], out_w_ref[:, cols])
        edge_ref[:, cols] = (first_ref[:, cols] + gate_ref[:, cols] * projected).astype(BF16)
    head = pltpu.make_async_copy(edge_ref.at[pl.ds(0, HALO)], next_ref.at[pl.ds(0, HALO)], sems.at[1])
    tail = pltpu.make_async_copy(
        edge_ref.at[pl.ds(HALO, HALO)], next_ref.at[pl.ds(frames - HALO, HALO)], sems.at[2]
    )
    head.start()
    tail.start()
    inner.wait()
    head.wait()
    tail.wait()


def close_call(
    near, prompt, mixed, keyed, gram, bias, query, key, value, sums, totals, first, gate, out_w, done
):
    frames, width = query.shape
    return pl.pallas_call(
        close_kernel,
        in_specs=[whole()] * 15,
        out_specs=whole(pltpu.HBM),
        out_shape=jax.ShapeDtypeStruct((frames, width), BF16),
        scratch_shapes=[
            pltpu.VMEM((width, 2 * HALO), BF16),
            pltpu.VMEM((2 * HALO, 2 * width), BF16),
            pltpu.VMEM((2 * TILE, width), BF16),
            pltpu.VMEM((2 * TILE, width), BF16),
            pltpu.SemaphoreType.DMA((3,)),
        ],
        compiler_params=pltpu.CompilerParams(vmem_limit_bytes=VMEM_LIMIT),
        cost_estimate=pl.CostEstimate(
            flops=2_000_000_000, bytes_accessed=6_000_000, transcendentals=1_000_000
        ),
        name="close",
    )(near, prompt, mixed, keyed, gram, bias, query, key, value, sums, totals, first, gate, out_w, done)


def body(
    hidden,
    latent,
    prompt_mel,
    window_back,
    window_ahead,
    step_index,
    proj_weight,
    latent_weight,
    prompt_weight,
    time_weight,
    qkv_weight,
    attn_out_weight,
):
    axes = ("seq", "cfg")
    spans = lax.axis_size("seq")
    mel = latent.shape[0]
    total_blocks = 2 * spans * (hidden.shape[0] // BLK)

    def at(span, cell):
        return span * 4 + cell

    everyone = [(span, cell) for span in range(spans) for cell in range(4)]
    to_partner = [(at(s, c), at(s, c ^ 1)) for s, c in everyone]
    to_half = [(at(s, c), at(s, c ^ 3)) for s, c in everyone]
    to_span = [
        (at(s, c), at(s + (1 if c >= 2 else -1), c))
        for s, c in everyone
        if 0 <= s + (1 if c >= 2 else -1) < spans
    ]
    vel, sent = velocity_call(hidden, proj_weight.T)
    sent, step_index = lax.optimization_barrier((sent, step_index))
    partner = lax.ppermute(sent, axes, to_partner)
    delta = time_value(step_index + 1) - time_value(step_index)
    feats = time_features(step_index, time_weight.shape[0])
    mixed, keyed, gram, embed, gate, bias = prepare_call(
        total_blocks,
        window_back,
        window_ahead,
        feats,
        latent_weight,
        prompt_weight,
        time_weight,
        qkv_weight,
    )
    partner, gate = lax.optimization_barrier((partner, gate))
    latent_out, own, far, cross = combine_call(delta, vel, partner, latent, prompt_mel)
    relayed = lax.ppermute(far, axes, to_span)
    query, key, value, context = inner_call(mel, own, mixed, keyed, gram, bias)
    near = jnp.concatenate([cross, relayed], axis=0)
    near, context = lax.optimization_barrier((near, context))
    near = lax.ppermute(near, axes, to_half)
    done, first, sums, totals = outer_call(
        own, query, key, value, bias, context, embed, gate, attn_out_weight
    )
    hidden_next = close_call(
        near,
        prompt_mel,
        mixed,
        keyed,
        gram,
        bias,
        query,
        key,
        value,
        sums,
        totals,
        first,
        gate,
        attn_out_weight,
        done,
    )
    return (latent_out, hidden_next)


def solution(mesh):
    in_specs = (
        P(("seq", "cfg"), None),
        P(None, "seq"),
        P(None, "seq"),
        P("seq"),
        P("seq"),
        P(),
        P(),
        P(),
        P(),
        P(),
        P(),
        P(),
    )
    out_specs = (P(None, ("seq", "cfg")), P(("seq", "cfg"), None))
    return jax.shard_map(body, mesh=mesh, in_specs=in_specs, out_specs=out_specs, check_vma=False)
```

```python
import functools
import math

import jax
import jax.numpy as jnp
from jax import lax
from jax.experimental import pallas as pl
from jax.experimental.pallas import tpu as pltpu
from jax.sharding import PartitionSpec as P

HEADS = 16
BLK = 32
NSTEPS = 32
HALO = 128
EPS = 1e-06
GUIDE = 0.5
TILE = 128
MASKED = -1e30
SMALL = 1e-30
LARGE = 1e30

F32 = jnp.float32
BF16 = jnp.bfloat16
VMEM_LIMIT = 24 * 1024 * 1024
SMALL_VMEM = 8 * 1024 * 1024


def mm(a, b):
    return jnp.dot(a, b, preferred_element_type=F32)


def mm_nt(a, b):
    return lax.dot_general(a, b, (((1,), (1,)), ((), ())), preferred_element_type=F32)


def whole(memory_space=pltpu.VMEM):
    return pl.BlockSpec(memory_space=memory_space)


def in_hbm(array):
    return pltpu.with_memory_space_constraint(array, pltpu.HBM)


def location():
    place = lax.axis_index("cfg")
    half = place // 2
    return half, place % 2, 2 * lax.axis_index("seq") + half


def sin_cos(angle):
    turns = jnp.floor(angle * (2.0 / math.pi) + 0.5)
    rest = angle - turns * 1.5703125
    rest = rest - turns * 4.837512969970703125e-4
    rest = rest - turns * 7.549789954891882e-8
    square = rest * rest
    sine = rest + rest * square * (
        -1.6666654611e-1 + square * (8.3321608736e-3 - square * 1.9515295891e-4)
    )
    cosine = (
        1.0
        - 0.5 * square
        + square
        * square
        * (4.166664568298827e-2 + square * (-1.388731625493765e-3 + square * 2.443315711809948e-5))
    )
    quarter = turns - 4.0 * jnp.floor(turns * 0.25)
    odd = (quarter == 1.0) | (quarter == 3.0)
    sine, cosine = jnp.where(odd, cosine, sine), jnp.where(odd, sine, cosine)
    sine = jnp.where(quarter >= 2.0, -sine, sine)
    cosine = jnp.where((quarter == 1.0) | (quarter == 2.0), -cosine, cosine)
    return sine, cosine


def time_value(step):
    return 1.0 - sin_cos(0.5 * math.pi * step / NSTEPS)[1]


def time_features(step):
    later = time_value(step + 1.0)
    half_freq = step.shape[1] // 2
    lane = lax.broadcasted_iota(jnp.int32, step.shape, 1)
    which = jnp.where(lane < half_freq, lane, lane - half_freq).astype(F32)
    freqs = jnp.exp(-math.log(10000.0) * which / half_freq)
    sine, cosine = sin_cos(1000.0 * later * freqs)
    return jnp.where(lane < half_freq, sine, cosine)


def velocity_kernel(hidden_ref, weight_ref, vel_ref, sent_ref, rows_ref, held_ref, sems):
    parts = sems.shape[0] - 1
    size = hidden_ref.shape[0] // parts
    copies = []
    for part in range(parts):
        here = pl.ds(part * size, size)
        copies.append(
            pltpu.make_async_copy(hidden_ref.at[here], rows_ref.at[here], sems.at[part])
        )
    copies.append(pltpu.make_async_copy(weight_ref, held_ref, sems.at[parts]))
    for copy in reversed(copies):
        copy.start()
    copies[parts].wait()
    weight = held_ref[...]
    for copy in copies[:parts]:
        copy.wait()
    for part in range(parts):
        here = slice(part * size, (part + 1) * size)
        rows = rows_ref[here].astype(F32)
        mean = jnp.mean(rows, axis=-1, keepdims=True)
        centered = rows - mean
        spread = jnp.mean(centered * centered, axis=-1, keepdims=True)
        normed = (centered * lax.rsqrt(spread + EPS)).astype(BF16)
        vel = mm_nt(weight, normed)
        vel_ref[:, here] = vel
        sent_ref[:, here] = vel.astype(BF16)


def velocity_call(hidden, proj_turned):
    rows, width = hidden.shape
    mel = proj_turned.shape[0]
    return pl.pallas_call(
        velocity_kernel,
        in_specs=[whole(pltpu.HBM)] * 2,
        out_specs=[whole()] * 2,
        out_shape=[
            jax.ShapeDtypeStruct((mel, rows), F32),
            jax.ShapeDtypeStruct((mel, rows), BF16),
        ],
        scratch_shapes=[
            pltpu.VMEM((rows, width), BF16),
            pltpu.VMEM((mel, width), BF16),
            pltpu.SemaphoreType.DMA((5,)),
        ],
        compiler_params=pltpu.CompilerParams(vmem_limit_bytes=SMALL_VMEM),
        cost_estimate=pl.CostEstimate(
            flops=10_000_000_000, bytes_accessed=2 * rows * width, transcendentals=0
        ),
        name="velocity",
    )(in_hbm(hidden), in_hbm(proj_turned))


def prepare_kernel(
    total_blocks,
    step_ref,
    back_hbm,
    ahead_hbm,
    latent_w_hbm,
    prompt_w_hbm,
    time_w_ref,
    qkv_ref,
    mixed_ref,
    keyed_ref,
    gram_ref,
    embed_ref,
    gate_ref,
    bias_ref,
    delta_ref,
    left_ref,
    back_ref,
    ahead_ref,
    latent_w_ref,
    prompt_w_ref,
    sems,
):
    mel, width = latent_w_ref.shape
    small = [
        pltpu.make_async_copy(source, target, sems.at[index])
        for index, (source, target) in enumerate(
            [
                (latent_w_hbm, latent_w_ref),
                (prompt_w_hbm, prompt_w_ref),
                (back_hbm, back_ref),
                (ahead_hbm, ahead_ref),
            ]
        )
    ]
    parts = 3
    columns = 3 * width // parts
    for copy in small:
        copy.start()

    small[0].wait()
    small[1].wait()
    both = jnp.concatenate([latent_w_ref[...], prompt_w_ref[...]], axis=0)
    wide = both.astype(F32)
    centered = wide - jnp.mean(wide, axis=-1, keepdims=True)
    embed = jnp.concatenate(
        [both, latent_w_ref[...], jnp.zeros((256 - 3 * mel, width), BF16)], axis=0
    )
    embed_ref[...] = embed
    col = jnp.mean(embed.astype(F32), axis=-1, keepdims=True)
    row = mm_nt(jnp.ones((16, width), BF16), embed)[0:1] / width
    gram = mm_nt(embed, embed) / width - col * row
    gram_high = gram.astype(BF16)
    gram_ref[0:256] = gram_high
    gram_ref[256:512] = (gram - gram_high.astype(F32)).astype(BF16)

    step = jnp.full((1, time_w_ref.shape[0]), step_ref[0], jnp.int32).astype(F32)
    feats = jnp.broadcast_to(time_features(step), (16, step.shape[1]))
    step = step[:, :128]
    delta_ref[...] = time_value(step + 1.0) - time_value(step)
    high = feats.astype(BF16)
    rest = feats - high.astype(F32)
    mid = rest.astype(BF16)
    low = (rest - mid.astype(F32)).astype(BF16)
    pieces = mm(jnp.concatenate([high, mid, low], axis=0), time_w_ref[...])
    mod = pieces[0:1] + (pieces[16:17] + pieces[32:33])
    shift, scale, gate = mod[:, :width], mod[:, width : 2 * width], mod[:, 2 * width :]
    gate_ref[...] = gate
    left_ref[0 : 2 * mel] = (centered * (1.0 + scale)).astype(BF16)
    shift_high = shift.astype(BF16).astype(F32)
    which = lax.broadcasted_iota(jnp.int32, (16, width), 0)
    left_ref[2 * mel : 2 * mel + 16] = jnp.where(
        which == 0, shift_high, jnp.where(which == 1, shift - shift_high, 0.0)
    ).astype(BF16)

    small[2].wait()
    small[3].wait()
    half, _, span = location()
    per_half = back_ref.shape[0] // 2
    keys = bias_ref.shape[1]
    row_block = lax.broadcasted_iota(jnp.int32, (16, keys), 0)
    lower = jnp.zeros((16, keys), jnp.int32)
    upper = jnp.zeros((16, keys), jnp.int32)
    for block in range(per_half):
        lower = jnp.where(row_block == block, block - back_ref[half * per_half + block], lower)
        upper = jnp.where(row_block == block, block + ahead_ref[half * per_half + block], upper)
    key_block = lax.broadcasted_iota(jnp.int32, (16, keys), 1) // BLK - HALO // BLK
    place = key_block + span * per_half
    seen = (key_block >= lower) & (key_block <= upper) & (place >= 0) & (place < total_blocks)
    bias_ref[0:16] = jnp.where(seen, 0.0, MASKED).astype(BF16)
    bias_ref[16:128] = jnp.zeros((112, keys), BF16)

    left = left_ref[...]
    for part in range(parts):
        start = part * columns
        acc = mm(left, qkv_ref[:, start : start + columns])
        if start < width:
            acc = acc * (math.log2(math.e) / math.sqrt(width // HEADS))
        offset = acc[2 * mel : 2 * mel + 1] + acc[2 * mel + 1 : 2 * mel + 2]
        offset_high = offset.astype(BF16).astype(F32)
        which = lax.broadcasted_iota(jnp.int32, (256 - 3 * mel, columns), 0)
        last = jnp.where(which == 0, offset_high, jnp.where(which == 1, offset - offset_high, 0.0))
        block = jnp.concatenate([acc[: 2 * mel], acc[:mel], last], axis=0).astype(BF16)
        if start < width:
            mixed_ref[:, start : start + columns] = block
        elif start < 2 * width:
            keyed_ref[start - width : start - width + columns] = block.T
        else:
            mixed_ref[:, start - width : start - width + columns] = block


def prepare_call(
    total_blocks, step_index, back, ahead, latent_weight, prompt_weight, time_weight, qkv_weight
):
    mel, width = latent_weight.shape
    return pl.pallas_call(
        functools.partial(prepare_kernel, total_blocks),
        in_specs=[whole(pltpu.SMEM)] + [whole(pltpu.HBM)] * 4 + [whole()] * 2,
        out_specs=[whole()] * 7,
        out_shape=[
            jax.ShapeDtypeStruct((256, 2 * width), BF16),
            jax.ShapeDtypeStruct((width, 256), BF16),
            jax.ShapeDtypeStruct((512, 256), BF16),
            jax.ShapeDtypeStruct((256, width), BF16),
            jax.ShapeDtypeStruct((1, width), F32),
            jax.ShapeDtypeStruct((128, 512 + 2 * HALO), BF16),
            jax.ShapeDtypeStruct((1, 128), F32),
        ],
        scratch_shapes=[
            pltpu.VMEM((2 * mel + 16, width), BF16),
            pltpu.SMEM(back.shape, jnp.int32),
            pltpu.SMEM(ahead.shape, jnp.int32),
            pltpu.VMEM(latent_weight.shape, BF16),
            pltpu.VMEM(prompt_weight.shape, BF16),
            pltpu.SemaphoreType.DMA((4,)),
        ],
        compiler_params=pltpu.CompilerParams(vmem_limit_bytes=VMEM_LIMIT),
        cost_estimate=pl.CostEstimate(
            flops=2 * 256 * width * 3 * width, bytes_accessed=8 * width * width, transcendentals=0
        ),
        name="prepare",
    )(
        step_index,
        in_hbm(back),
        in_hbm(ahead),
        in_hbm(latent_weight),
        in_hbm(prompt_weight),
        time_weight,
        qkv_weight,
    )


def weights_of(delta_ref):
    branch = lax.axis_index("cfg") % 2
    delta = delta_ref[0:1, 0:1]
    mine = jnp.where(branch == 0, 1.0 + GUIDE, -GUIDE) * delta
    other = jnp.where(branch == 0, -GUIDE, 1.0 + GUIDE) * delta
    return mine, other


def updated_end(refs, half, own, whole_block):
    delta_ref, vel_ref, partner_ref, latent_ref = refs

    def ends(ref, places):
        head, tail = places
        return jnp.where(half == 0, ref[:, head : head + HALO], ref[:, tail : tail + HALO])

    mine, other = weights_of(delta_ref)
    return (
        ends(latent_ref, whole_block)
        + (mine * ends(vel_ref, own) + other * ends(partner_ref, own).astype(F32))
    ).astype(BF16)


def far_kernel(delta_ref, vel_ref, partner_ref, latent_ref, prompt_ref, far_ref):
    half, _, _ = location()
    mel, frames = vel_ref.shape
    last = 2 * frames - HALO
    far_ref[0:mel] = updated_end(
        (delta_ref, vel_ref, partner_ref, latent_ref), half, (0, frames - HALO), (0, last)
    )
    far_ref[mel : 2 * mel] = jnp.where(
        half == 0, prompt_ref[:, :HALO], prompt_ref[:, last:]
    ).astype(BF16)


def combine_kernel(
    delta_ref, vel_ref, partner_ref, latent_ref, prompt_ref, next_ref, rows_ref, cross_ref
):
    half, branch, _ = location()
    mel, frames = vel_ref.shape
    mine, other = weights_of(delta_ref)
    latent = jnp.where(half == 0, latent_ref[:, :frames], latent_ref[:, frames:])
    prompt = jnp.where(half == 0, prompt_ref[:, :frames], prompt_ref[:, frames:])
    updated = latent + (mine * vel_ref[...] + other * partner_ref[...].astype(F32))
    head, tail = updated[:, :HALO], updated[:, frames - HALO :]
    cross_ref[...] = jnp.where(half == 0, tail, head).astype(BF16)
    share = frames // 2
    next_ref[...] = jnp.where(branch == 0, updated[:, :share], updated[:, share:])
    high = updated.astype(BF16)
    rows_ref[0:mel] = high
    rows_ref[mel : 2 * mel] = jnp.where(branch == 0, prompt, 0.0).astype(BF16)
    rows_ref[2 * mel : 3 * mel] = (updated - high.astype(F32)).astype(BF16)
    rows_ref[3 * mel : 256] = jnp.zeros((256 - 3 * mel, frames), BF16)


def combine_call(delta, vel, partner, latent, prompt):
    mel, frames = vel.shape
    return pl.pallas_call(
        combine_kernel,
        in_specs=[whole()] * 5,
        out_specs=[whole()] * 3,
        out_shape=[
            jax.ShapeDtypeStruct((mel, frames // 2), F32),
            jax.ShapeDtypeStruct((256, frames), BF16),
            jax.ShapeDtypeStruct((mel, HALO), BF16),
        ],
        compiler_params=pltpu.CompilerParams(vmem_limit_bytes=SMALL_VMEM),
        cost_estimate=pl.CostEstimate(
            flops=5_000_000_000, bytes_accessed=1_000_000, transcendentals=0
        ),
        name="combine",
    )(delta, vel, partner, latent, prompt)


def far_call(delta, vel, partner, latent, prompt):
    return pl.pallas_call(
        far_kernel,
        in_specs=[whole()] * 5,
        out_specs=whole(),
        out_shape=jax.ShapeDtypeStruct((2 * vel.shape[0], HALO), BF16),
        compiler_params=pltpu.CompilerParams(vmem_limit_bytes=SMALL_VMEM),
        name="far",
    )(delta, vel, partner, latent, prompt)


def normalised(rows, gram_ref, mel):
    weighted = mm(gram_ref[0:256], rows) + mm(gram_ref[256:512], rows)
    rows = rows.astype(F32)
    spread = jnp.sum(weighted * rows, axis=0, keepdims=True)
    inverse = lax.rsqrt(jnp.maximum(spread, 0.0) + EPS)
    latent = (rows[0:mel] + rows[2 * mel : 3 * mel]) * inverse
    high = latent.astype(BF16)
    which = lax.broadcasted_iota(jnp.int32, (256 - 3 * mel, rows.shape[1]), 0)
    return jnp.concatenate(
        [
            high,
            (rows[mel : 2 * mel] * inverse).astype(BF16),
            (latent - high.astype(F32)).astype(BF16),
            jnp.where(which < 2, 1.0, 0.0).astype(BF16),
        ],
        axis=0,
    )


def split_values(values, start, value_ref):
    left = lax.broadcasted_iota(jnp.int32, (values.shape[0], 128), 1) < 64
    for part in range(2):
        pair = values[:, 128 * part : 128 * (part + 1)]
        at = 2 * start + 256 * part
        value_ref[:, at : at + 128] = jnp.where(left, pair, 0.0).astype(BF16)
        value_ref[:, at + 128 : at + 256] = jnp.where(left, 0.0, pair).astype(BF16)


def pair_queries(query, tile):
    row = lax.broadcasted_iota(jnp.int32, (TILE, 128), 0)
    lane = lax.broadcasted_iota(jnp.int32, (TILE, 128), 1)
    chosen = (lane == tile * (TILE // BLK) + row // BLK).astype(F32).astype(BF16)
    return jnp.concatenate([query, chosen], axis=1)


def pair_scores(queries, key_left, key_right, bias):
    gap = jnp.zeros_like(key_left)
    key = jnp.concatenate(
        [
            jnp.concatenate([key_left, gap, bias], axis=0),
            jnp.concatenate([gap, key_right, bias], axis=0),
        ],
        axis=1,
    )
    return mm(queries, key)


def pair_sums(scores, value_left, value_right):
    left = lax.broadcasted_iota(jnp.int32, value_left.shape, 1) < 64
    ones_left = jnp.where(left, 1.0, 0.0).astype(BF16)
    ones_right = jnp.where(left, 0.0, 1.0).astype(BF16)
    value = jnp.concatenate(
        [
            jnp.concatenate([value_left, ones_left], axis=1),
            jnp.concatenate([value_right, ones_right], axis=1),
        ],
        axis=0,
    )
    return mm(jnp.exp2(scores).astype(BF16), value)


def less_top(scores, tops):
    size = scores.shape[1] // 2
    return jnp.concatenate([scores[:, :size] - tops[0], scores[:, size:] - tops[1]], axis=1)


def top_of(scores):
    size = scores.shape[1] // 2
    return (
        jnp.max(scores[:, :size], axis=-1, keepdims=True),
        jnp.max(scores[:, size:], axis=-1, keepdims=True),
    )


def in_range(least, most):
    return (jnp.min(least) > SMALL) & (jnp.max(most) < LARGE)


def pair_keys(key_ref, pair, window):
    return (
        key_ref[pl.ds(pair * 128, 64), window],
        key_ref[pl.ds(pair * 128 + 64, 64), window],
    )


def pair_values(value_ref, pair, window):
    return (
        value_ref[window, pl.ds(pair * 256, 128)],
        value_ref[window, pl.ds(pair * 256 + 128, 128)],
    )


def edges_of(frames):
    own = TILE + HALO
    return (
        (0, 0, 0, HALO, 0),
        (frames // TILE - 1, frames - own, HALO, frames + HALO - own, frames + HALO),
    )


def layer_kernel(
    mel,
    own_ref,
    mixed_ref,
    keyed_ref,
    gram_ref,
    bias_ref,
    embed_ref,
    gate_ref,
    out_w_ref,
    query_ref,
    key_ref,
    value_ref,
    done_ref,
    first_ref,
    sums_ref,
    totals_ref,
    context_ref,
):
    frames, width = query_ref.shape
    pairs = width // 128
    own = own_ref[...]
    normed = normalised(own, gram_ref, mel)
    turned = normed.T
    for start in range(0, width, 256):
        cols = slice(start, start + 256)
        key_ref[cols] = mm(keyed_ref[cols], normed).astype(BF16)
        query_ref[:, cols] = mm(turned, mixed_ref[:, cols]).astype(BF16)
        split_values(
            mm(turned, mixed_ref[:, width + start : width + start + 256]), start, value_ref
        )

    def attend(tile, pair, stable):
        at = tile * TILE
        cols = pl.ds(pair * 128, 128)
        window = pl.ds(at - HALO, TILE + 2 * HALO)
        queries = pair_queries(query_ref[pl.ds(at, TILE), cols], tile)
        scores = pair_scores(
            queries, *pair_keys(key_ref, pair, window), bias_ref[:, pl.ds(at, TILE + 2 * HALO)]
        )
        if stable:
            scores = less_top(scores, top_of(scores))
        sums = pair_sums(scores, *pair_values(value_ref, pair, window))
        total = sums[:, 128:]
        context_ref[pl.ds(at - HALO, TILE), cols] = (sums[:, :128] / total).astype(BF16)
        return total

    first, last = HALO // TILE, (frames - HALO) // TILE
    least = jnp.full((TILE, 128), 1.0, F32)
    most = jnp.full((TILE, 128), 1.0, F32)
    for tile in range(first, last):
        for pair in range(pairs):
            total = attend(tile, pair, False)
            least = jnp.minimum(least, total)
            most = jnp.maximum(most, total)
    for edge, (tile, at, _, bias_at, _) in enumerate(edges_of(frames)):
        window = pl.ds(at, TILE + HALO)
        here = slice(edge * TILE, (edge + 1) * TILE)
        for pair in range(pairs):
            cols = slice(pair * 128, (pair + 1) * 128)
            queries = pair_queries(query_ref[tile * TILE : (tile + 1) * TILE, cols], tile)
            scores = pair_scores(
                queries,
                *pair_keys(key_ref, pair, window),
                bias_ref[:, bias_at : bias_at + TILE + HALO],
            )
            sums = pair_sums(scores, *pair_values(value_ref, pair, window))
            sums_ref[here, cols] = sums[:, :128]
            totals_ref[here, cols] = sums[:, 128:]

    @pl.when(jnp.logical_not(in_range(least, most)))
    def _():
        def one(index, carry):
            attend(first + index // pairs, index % pairs, True)
            return carry

        lax.fori_loop(0, (last - first) * pairs, one, 0)

    own_turned = own.T
    for start in range(0, width, 256):
        cols = slice(start, start + 256)
        start_rows = mm(own_turned, embed_ref[:, cols])
        projected = mm(context_ref[...], out_w_ref[:, cols])
        done_ref[:, cols] = (
            start_rows[HALO : frames - HALO] + gate_ref[:, cols] * projected
        ).astype(BF16)
        first_ref[0:HALO, cols] = start_rows[0:HALO]
        first_ref[HALO : 2 * HALO, cols] = start_rows[frames - HALO :]


def layer_call(mel, own, mixed, keyed, gram, bias, embed, gate, out_w):
    frames = own.shape[1]
    width = out_w.shape[0]
    return pl.pallas_call(
        functools.partial(layer_kernel, mel),
        in_specs=[whole()] * 8,
        out_specs=[whole()] * 7,
        out_shape=[
            jax.ShapeDtypeStruct((frames, width), BF16),
            jax.ShapeDtypeStruct((width, frames), BF16),
            jax.ShapeDtypeStruct((frames, 2 * width), BF16),
            jax.ShapeDtypeStruct((frames - 2 * HALO, width), BF16),
            jax.ShapeDtypeStruct((2 * HALO, width), F32),
            jax.ShapeDtypeStruct((2 * TILE, width), F32),
            jax.ShapeDtypeStruct((2 * TILE, width), F32),
        ],
        scratch_shapes=[pltpu.VMEM((frames - 2 * HALO, width), BF16)],
        compiler_params=pltpu.CompilerParams(vmem_limit_bytes=VMEM_LIMIT),
        cost_estimate=pl.CostEstimate(
            flops=5_000_000_000, bytes_accessed=6_000_000, transcendentals=2_000_000
        ),
        name="layer",
    )(own, mixed, keyed, gram, bias, embed, gate, out_w)


def close_kernel(
    far_ref,
    cross_ref,
    prompt_ref,
    mixed_ref,
    keyed_ref,
    gram_ref,
    bias_ref,
    query_ref,
    key_ref,
    value_ref,
    sums_ref,
    totals_ref,
    first_ref,
    gate_ref,
    out_w_ref,
    done_ref,
    next_ref,
    near_key_ref,
    near_value_ref,
    context_ref,
    edge_ref,
    sems,
):
    half, branch, _ = location()
    frames, width = query_ref.shape
    pairs = width // 128
    mel = cross_ref.shape[0]
    inner = pltpu.make_async_copy(done_ref, next_ref.at[pl.ds(HALO, frames - 2 * HALO)], sems.at[0])
    inner.start()
    flag = jnp.where(branch == 0, 1.0, 0.0)
    prompt = jnp.where(
        half == 0, prompt_ref[:, frames : frames + HALO], prompt_ref[:, frames - HALO : frames]
    )
    blank = jnp.zeros((256 - 2 * mel, HALO), F32)
    far = far_ref[...].astype(F32)
    cross_rows = jnp.concatenate([cross_ref[...].astype(F32), prompt * flag, blank], axis=0)
    seq_rows = jnp.concatenate([far[0:mel], far[mel:] * flag, blank], axis=0)
    before = jnp.where(half == 0, seq_rows, cross_rows).astype(BF16)
    after = jnp.where(half == 0, cross_rows, seq_rows).astype(BF16)
    normed = normalised(jnp.concatenate([before, after], axis=1), gram_ref, mel)
    turned = normed.T
    for start in range(0, width, 256):
        cols = slice(start, start + 256)
        near_key_ref[cols] = mm(keyed_ref[cols], normed).astype(BF16)
        split_values(
            mm(turned, mixed_ref[:, width + start : width + start + 256]), start, near_value_ref
        )

    edges = edges_of(frames)
    least = jnp.full((TILE, 128), 1.0, F32)
    most = jnp.full((TILE, 128), 1.0, F32)
    for edge, (tile, _, near_at, _, bias_at) in enumerate(edges):
        window = pl.ds(near_at, HALO)
        here = slice(edge * TILE, (edge + 1) * TILE)
        for pair in range(pairs):
            cols = slice(pair * 128, (pair + 1) * 128)
            queries = pair_queries(query_ref[tile * TILE : (tile + 1) * TILE, cols], tile)
            scores = pair_scores(
                queries,
                *pair_keys(near_key_ref, pair, window),
                bias_ref[:, bias_at : bias_at + HALO],
            )
            sums = pair_sums(scores, *pair_values(near_value_ref, pair, window))
            total = sums[:, 128:] + totals_ref[here, cols]
            context_ref[here, cols] = ((sums[:, :128] + sums_ref[here, cols]) / total).astype(BF16)
            least = jnp.minimum(least, total)
            most = jnp.maximum(most, total)

    @pl.when(jnp.logical_not(in_range(least, most)))
    def _():
        for edge, (tile, at, near_at, bias_own, bias_near) in enumerate(edges):
            here = slice(edge * TILE, (edge + 1) * TILE)

            def one(pair, carry):
                cols = pl.ds(pair * 128, 128)
                own_window = pl.ds(at, TILE + HALO)
                near_window = pl.ds(near_at, HALO)
                queries = pair_queries(query_ref[tile * TILE : (tile + 1) * TILE, cols], tile)
                own_scores = pair_scores(
                    queries,
                    *pair_keys(key_ref, pair, own_window),
                    bias_ref[:, bias_own : bias_own + TILE + HALO],
                )
                near_scores = pair_scores(
                    queries,
                    *pair_keys(near_key_ref, pair, near_window),
                    bias_ref[:, bias_near : bias_near + HALO],
                )
                tops = [
                    jnp.maximum(a, b) for a, b in zip(top_of(own_scores), top_of(near_scores))
                ]
                sums = pair_sums(
                    less_top(own_scores, tops), *pair_values(value_ref, pair, own_window)
                ) + pair_sums(
                    less_top(near_scores, tops), *pair_values(near_value_ref, pair, near_window)
                )
                context_ref[here, cols] = (sums[:, :128] / sums[:, 128:]).astype(BF16)
                return carry

            lax.fori_loop(0, pairs, one, 0)

    for start in range(0, width, 256):
        cols = slice(start, start + 256)
        projected = mm(context_ref[...], out_w_ref[:, cols])
        edge_ref[:, cols] = (first_ref[:, cols] + gate_ref[:, cols] * projected).astype(BF16)
    head = pltpu.make_async_copy(edge_ref.at[pl.ds(0, HALO)], next_ref.at[pl.ds(0, HALO)], sems.at[1])
    tail = pltpu.make_async_copy(
        edge_ref.at[pl.ds(HALO, HALO)], next_ref.at[pl.ds(frames - HALO, HALO)], sems.at[2]
    )
    head.start()
    tail.start()
    inner.wait()
    head.wait()
    tail.wait()


def close_call(
    far, cross, prompt, mixed, keyed, gram, bias, query, key, value, sums, totals, first, gate, out_w, done
):
    frames, width = query.shape
    return pl.pallas_call(
        close_kernel,
        in_specs=[whole()] * 16,
        out_specs=whole(pltpu.HBM),
        out_shape=jax.ShapeDtypeStruct((frames, width), BF16),
        scratch_shapes=[
            pltpu.VMEM((width, 2 * HALO), BF16),
            pltpu.VMEM((2 * HALO, 2 * width), BF16),
            pltpu.VMEM((2 * TILE, width), BF16),
            pltpu.VMEM((2 * TILE, width), BF16),
            pltpu.SemaphoreType.DMA((3,)),
        ],
        compiler_params=pltpu.CompilerParams(vmem_limit_bytes=VMEM_LIMIT),
        cost_estimate=pl.CostEstimate(
            flops=2_000_000_000, bytes_accessed=6_000_000, transcendentals=1_000_000
        ),
        name="close",
    )(
        far,
        cross,
        prompt,
        mixed,
        keyed,
        gram,
        bias,
        query,
        key,
        value,
        sums,
        totals,
        first,
        gate,
        out_w,
        done,
    )


def body(
    hidden,
    latent,
    prompt_mel,
    window_back,
    window_ahead,
    step_index,
    proj_weight,
    latent_weight,
    prompt_weight,
    time_weight,
    qkv_weight,
    attn_out_weight,
):
    axes = ("seq", "cfg")
    spans = lax.axis_size("seq")
    total_blocks = 2 * spans * (hidden.shape[0] // BLK)

    def at(span, cell):
        return span * 4 + cell

    everyone = [(span, cell) for span in range(spans) for cell in range(4)]
    to_partner = [(at(s, c), at(s, c ^ 1)) for s, c in everyone]
    to_half = [(at(s, c), at(s, c ^ 3)) for s, c in everyone]
    to_span = [
        (at(s, c), at(s + (1 if c >= 2 else -1), c ^ 3))
        for s, c in everyone
        if 0 <= s + (1 if c >= 2 else -1) < spans
    ]
    vel, sent = velocity_call(hidden, proj_weight.T)
    sent, step_index = lax.optimization_barrier((sent, step_index))
    partner = lax.ppermute(sent, axes, to_partner)
    mixed, keyed, gram, embed, gate, bias, delta = prepare_call(
        total_blocks,
        step_index,
        window_back,
        window_ahead,
        latent_weight,
        prompt_weight,
        time_weight,
        qkv_weight,
    )
    far = far_call(delta, vel, partner, latent, prompt_mel)
    far = lax.ppermute(far, axes, to_span)
    latent_out, own, cross = combine_call(delta, vel, partner, latent, prompt_mel)
    cross = lax.ppermute(cross, axes, to_half)
    query, key, value, done, first, sums, totals = layer_call(
        latent.shape[0], own, mixed, keyed, gram, bias, embed, gate, attn_out_weight
    )
    hidden_next = close_call(
        far,
        cross,
        prompt_mel,
        mixed,
        keyed,
        gram,
        bias,
        query,
        key,
        value,
        sums,
        totals,
        first,
        gate,
        attn_out_weight,
        done,
    )
    return (latent_out, hidden_next)


def solution(mesh):
    in_specs = (
        P(("seq", "cfg"), None),
        P(None, "seq"),
        P(None, "seq"),
        P("seq"),
        P("seq"),
        P(),
        P(),
        P(),
        P(),
        P(),
        P(),
        P(),
    )
    out_specs = (P(None, ("seq", "cfg")), P(("seq", "cfg"), None))
    return jax.shard_map(body, mesh=mesh, in_specs=in_specs, out_specs=out_specs, check_vma=False)
```

```python
import functools
import math

import jax
import jax.numpy as jnp
from jax import lax
from jax.experimental import pallas as pl
from jax.experimental.pallas import tpu as pltpu
from jax.sharding import PartitionSpec as P

HEADS = 16
BLK = 32
NSTEPS = 32
HALO = 128
EPS = 1e-06
GUIDE = 0.5
TILE = 128
MASKED = -1e30
SMALL = 1e-30
LARGE = 1e30

F32 = jnp.float32
BF16 = jnp.bfloat16
VMEM_LIMIT = 24 * 1024 * 1024
SMALL_VMEM = 8 * 1024 * 1024


def mm(a, b):
    return jnp.dot(a, b, preferred_element_type=F32)


def mm_nt(a, b):
    return lax.dot_general(a, b, (((1,), (1,)), ((), ())), preferred_element_type=F32)


def whole(memory_space=pltpu.VMEM):
    return pl.BlockSpec(memory_space=memory_space)


def in_hbm(array):
    return pltpu.with_memory_space_constraint(array, pltpu.HBM)


def location():
    place = lax.axis_index("cfg")
    half = place // 2
    return half, place % 2, 2 * lax.axis_index("seq") + half


def sin_cos(angle):
    turns = jnp.floor(angle * (2.0 / math.pi) + 0.5)
    rest = angle - turns * 1.5703125
    rest = rest - turns * 4.837512969970703125e-4
    rest = rest - turns * 7.549789954891882e-8
    square = rest * rest
    sine = rest + rest * square * (
        -1.6666654611e-1 + square * (8.3321608736e-3 - square * 1.9515295891e-4)
    )
    cosine = (
        1.0
        - 0.5 * square
        + square
        * square
        * (4.166664568298827e-2 + square * (-1.388731625493765e-3 + square * 2.443315711809948e-5))
    )
    quarter = turns - 4.0 * jnp.floor(turns * 0.25)
    odd = (quarter == 1.0) | (quarter == 3.0)
    sine, cosine = jnp.where(odd, cosine, sine), jnp.where(odd, sine, cosine)
    sine = jnp.where(quarter >= 2.0, -sine, sine)
    cosine = jnp.where((quarter == 1.0) | (quarter == 2.0), -cosine, cosine)
    return sine, cosine


def time_value(step):
    return 1.0 - sin_cos(0.5 * math.pi * step / NSTEPS)[1]


def time_features(step):
    later = time_value(step + 1.0)
    half_freq = step.shape[1] // 2
    lane = lax.broadcasted_iota(jnp.int32, step.shape, 1)
    which = jnp.where(lane < half_freq, lane, lane - half_freq).astype(F32)
    freqs = jnp.exp(-math.log(10000.0) * which / half_freq)
    sine, cosine = sin_cos(1000.0 * later * freqs)
    return jnp.where(lane < half_freq, sine, cosine)


def velocity_kernel(hidden_ref, weight_ref, vel_ref, sent_ref, rows_ref, held_ref, sems):
    parts = sems.shape[0] - 1
    size = hidden_ref.shape[0] // parts
    copies = []
    for part in range(parts):
        here = pl.ds(part * size, size)
        copies.append(
            pltpu.make_async_copy(hidden_ref.at[here], rows_ref.at[here], sems.at[part])
        )
    copies.append(pltpu.make_async_copy(weight_ref, held_ref, sems.at[parts]))
    for copy in reversed(copies):
        copy.start()
    copies[parts].wait()
    weight = held_ref[...]
    for copy in copies[:parts]:
        copy.wait()
    for part in range(parts):
        here = slice(part * size, (part + 1) * size)
        rows = rows_ref[here].astype(F32)
        mean = jnp.mean(rows, axis=-1, keepdims=True)
        centered = rows - mean
        spread = jnp.mean(centered * centered, axis=-1, keepdims=True)
        normed = (centered * lax.rsqrt(spread + EPS)).astype(BF16)
        vel = mm_nt(weight, normed)
        vel_ref[:, here] = vel
        sent_ref[:, here] = vel.astype(BF16)


def velocity_call(hidden, proj_turned):
    rows, width = hidden.shape
    mel = proj_turned.shape[0]
    return pl.pallas_call(
        velocity_kernel,
        in_specs=[whole(pltpu.HBM)] * 2,
        out_specs=[whole()] * 2,
        out_shape=[
            jax.ShapeDtypeStruct((mel, rows), F32),
            jax.ShapeDtypeStruct((mel, rows), BF16),
        ],
        scratch_shapes=[
            pltpu.VMEM((rows, width), BF16),
            pltpu.VMEM((mel, width), BF16),
            pltpu.SemaphoreType.DMA((5,)),
        ],
        compiler_params=pltpu.CompilerParams(vmem_limit_bytes=SMALL_VMEM),
        cost_estimate=pl.CostEstimate(
            flops=10_000_000_000, bytes_accessed=2 * rows * width, transcendentals=0
        ),
        name="velocity",
    )(in_hbm(hidden), in_hbm(proj_turned))


def prepare_kernel(
    total_blocks,
    step_ref,
    back_hbm,
    ahead_hbm,
    latent_w_hbm,
    prompt_w_hbm,
    time_w_ref,
    qkv_ref,
    mixed_ref,
    keyed_ref,
    gram_ref,
    embed_ref,
    gate_ref,
    bias_ref,
    delta_ref,
    left_ref,
    back_ref,
    ahead_ref,
    latent_w_ref,
    prompt_w_ref,
    sems,
):
    mel, width = latent_w_ref.shape
    small = [
        pltpu.make_async_copy(source, target, sems.at[index])
        for index, (source, target) in enumerate(
            [
                (latent_w_hbm, latent_w_ref),
                (prompt_w_hbm, prompt_w_ref),
                (back_hbm, back_ref),
                (ahead_hbm, ahead_ref),
            ]
        )
    ]
    parts = 3
    columns = 3 * width // parts
    for copy in small:
        copy.start()

    small[0].wait()
    small[1].wait()
    both = jnp.concatenate([latent_w_ref[...], prompt_w_ref[...]], axis=0)
    wide = both.astype(F32)
    centered = wide - jnp.mean(wide, axis=-1, keepdims=True)
    embed = jnp.concatenate(
        [both, latent_w_ref[...], jnp.zeros((256 - 3 * mel, width), BF16)], axis=0
    )
    embed_ref[...] = embed
    col = jnp.mean(embed.astype(F32), axis=-1, keepdims=True)
    row = mm_nt(jnp.ones((16, width), BF16), embed)[0:1] / width
    gram = mm_nt(embed, embed) / width - col * row
    gram_high = gram.astype(BF16)
    gram_ref[0:256] = gram_high
    gram_ref[256:512] = (gram - gram_high.astype(F32)).astype(BF16)

    step = jnp.full((1, time_w_ref.shape[0]), step_ref[0], jnp.int32).astype(F32)
    feats = jnp.broadcast_to(time_features(step), (16, step.shape[1]))
    step = step[:, :128]
    delta_ref[...] = time_value(step + 1.0) - time_value(step)
    high = feats.astype(BF16)
    rest = feats - high.astype(F32)
    mid = rest.astype(BF16)
    low = (rest - mid.astype(F32)).astype(BF16)
    pieces = mm(jnp.concatenate([high, mid, low], axis=0), time_w_ref[...])
    mod = pieces[0:1] + (pieces[16:17] + pieces[32:33])
    shift, scale, gate = mod[:, :width], mod[:, width : 2 * width], mod[:, 2 * width :]
    gate_ref[...] = gate
    left_ref[0 : 2 * mel] = (centered * (1.0 + scale)).astype(BF16)
    shift_high = shift.astype(BF16).astype(F32)
    which = lax.broadcasted_iota(jnp.int32, (16, width), 0)
    left_ref[2 * mel : 2 * mel + 16] = jnp.where(
        which == 0, shift_high, jnp.where(which == 1, shift - shift_high, 0.0)
    ).astype(BF16)

    small[2].wait()
    small[3].wait()
    half, _, span = location()
    per_half = back_ref.shape[0] // 2
    keys = bias_ref.shape[1]
    row_block = lax.broadcasted_iota(jnp.int32, (16, keys), 0)
    lower = jnp.zeros((16, keys), jnp.int32)
    upper = jnp.zeros((16, keys), jnp.int32)
    for block in range(per_half):
        lower = jnp.where(row_block == block, block - back_ref[half * per_half + block], lower)
        upper = jnp.where(row_block == block, block + ahead_ref[half * per_half + block], upper)
    key_block = lax.broadcasted_iota(jnp.int32, (16, keys), 1) // BLK - HALO // BLK
    place = key_block + span * per_half
    seen = (key_block >= lower) & (key_block <= upper) & (place >= 0) & (place < total_blocks)
    bias_ref[0:16] = jnp.where(seen, 0.0, MASKED).astype(BF16)
    bias_ref[16:128] = jnp.zeros((112, keys), BF16)

    left = left_ref[...]
    for part in range(parts):
        start = part * columns
        acc = mm(left, qkv_ref[:, start : start + columns])
        if start < width:
            acc = acc * (math.log2(math.e) / math.sqrt(width // HEADS))
        offset = acc[2 * mel : 2 * mel + 1] + acc[2 * mel + 1 : 2 * mel + 2]
        offset_high = offset.astype(BF16).astype(F32)
        which = lax.broadcasted_iota(jnp.int32, (256 - 3 * mel, columns), 0)
        last = jnp.where(which == 0, offset_high, jnp.where(which == 1, offset - offset_high, 0.0))
        block = jnp.concatenate([acc[: 2 * mel], acc[:mel], last], axis=0).astype(BF16)
        if start < width:
            mixed_ref[:, start : start + columns] = block
        elif start < 2 * width:
            keyed_ref[start - width : start - width + columns] = block.T
        else:
            mixed_ref[:, start - width : start - width + columns] = block


def prepare_call(
    total_blocks, step_index, back, ahead, latent_weight, prompt_weight, time_weight, qkv_weight
):
    mel, width = latent_weight.shape
    return pl.pallas_call(
        functools.partial(prepare_kernel, total_blocks),
        in_specs=[whole(pltpu.SMEM)] + [whole(pltpu.HBM)] * 4 + [whole()] * 2,
        out_specs=[whole()] * 7,
        out_shape=[
            jax.ShapeDtypeStruct((256, 2 * width), BF16),
            jax.ShapeDtypeStruct((width, 256), BF16),
            jax.ShapeDtypeStruct((512, 256), BF16),
            jax.ShapeDtypeStruct((256, width), BF16),
            jax.ShapeDtypeStruct((1, width), F32),
            jax.ShapeDtypeStruct((128, 512 + 2 * HALO), BF16),
            jax.ShapeDtypeStruct((1, 128), F32),
        ],
        scratch_shapes=[
            pltpu.VMEM((2 * mel + 16, width), BF16),
            pltpu.SMEM(back.shape, jnp.int32),
            pltpu.SMEM(ahead.shape, jnp.int32),
            pltpu.VMEM(latent_weight.shape, BF16),
            pltpu.VMEM(prompt_weight.shape, BF16),
            pltpu.SemaphoreType.DMA((4,)),
        ],
        compiler_params=pltpu.CompilerParams(vmem_limit_bytes=VMEM_LIMIT),
        cost_estimate=pl.CostEstimate(
            flops=2 * 256 * width * 3 * width, bytes_accessed=8 * width * width, transcendentals=0
        ),
        name="prepare",
    )(
        step_index,
        in_hbm(back),
        in_hbm(ahead),
        in_hbm(latent_weight),
        in_hbm(prompt_weight),
        time_weight,
        qkv_weight,
    )


def weights_of(delta_ref):
    branch = lax.axis_index("cfg") % 2
    delta = delta_ref[0:1, 0:1]
    mine = jnp.where(branch == 0, 1.0 + GUIDE, -GUIDE) * delta
    other = jnp.where(branch == 0, -GUIDE, 1.0 + GUIDE) * delta
    return mine, other


def updated_end(refs, half, own, whole_block):
    delta_ref, vel_ref, partner_ref, latent_ref = refs

    def ends(ref, places):
        head, tail = places
        return jnp.where(half == 0, ref[:, head : head + HALO], ref[:, tail : tail + HALO])

    mine, other = weights_of(delta_ref)
    return (
        ends(latent_ref, whole_block)
        + (mine * ends(vel_ref, own) + other * ends(partner_ref, own).astype(F32))
    ).astype(BF16)


def far_kernel(delta_ref, vel_ref, partner_ref, latent_ref, prompt_ref, far_ref):
    half, _, _ = location()
    mel, frames = vel_ref.shape
    last = 2 * frames - HALO
    far_ref[0:mel] = updated_end(
        (delta_ref, vel_ref, partner_ref, latent_ref), half, (0, frames - HALO), (0, last)
    )
    far_ref[mel : 2 * mel] = jnp.where(
        half == 0, prompt_ref[:, :HALO], prompt_ref[:, last:]
    ).astype(BF16)


def combine_kernel(
    delta_ref, vel_ref, partner_ref, latent_ref, prompt_ref, next_ref, rows_ref, cross_ref
):
    half, branch, _ = location()
    mel, frames = vel_ref.shape
    mine, other = weights_of(delta_ref)
    latent = jnp.where(half == 0, latent_ref[:, :frames], latent_ref[:, frames:])
    prompt = jnp.where(half == 0, prompt_ref[:, :frames], prompt_ref[:, frames:])
    updated = latent + (mine * vel_ref[...] + other * partner_ref[...].astype(F32))
    head, tail = updated[:, :HALO], updated[:, frames - HALO :]
    cross_ref[...] = jnp.where(half == 0, tail, head).astype(BF16)
    share = frames // 2
    next_ref[...] = jnp.where(branch == 0, updated[:, :share], updated[:, share:])
    high = updated.astype(BF16)
    rows_ref[0:mel] = high
    rows_ref[mel : 2 * mel] = jnp.where(branch == 0, prompt, 0.0).astype(BF16)
    rows_ref[2 * mel : 3 * mel] = (updated - high.astype(F32)).astype(BF16)
    rows_ref[3 * mel : 256] = jnp.zeros((256 - 3 * mel, frames), BF16)


def combine_call(delta, vel, partner, latent, prompt):
    mel, frames = vel.shape
    return pl.pallas_call(
        combine_kernel,
        in_specs=[whole()] * 5,
        out_specs=[whole()] * 3,
        out_shape=[
            jax.ShapeDtypeStruct((mel, frames // 2), F32),
            jax.ShapeDtypeStruct((256, frames), BF16),
            jax.ShapeDtypeStruct((mel, HALO), BF16),
        ],
        compiler_params=pltpu.CompilerParams(vmem_limit_bytes=SMALL_VMEM),
        cost_estimate=pl.CostEstimate(
            flops=5_000_000_000, bytes_accessed=1_000_000, transcendentals=0
        ),
        name="combine",
    )(delta, vel, partner, latent, prompt)


def far_call(delta, vel, partner, latent, prompt):
    return pl.pallas_call(
        far_kernel,
        in_specs=[whole()] * 5,
        out_specs=whole(),
        out_shape=jax.ShapeDtypeStruct((2 * vel.shape[0], HALO), BF16),
        compiler_params=pltpu.CompilerParams(vmem_limit_bytes=SMALL_VMEM),
        name="far",
    )(delta, vel, partner, latent, prompt)


def normalised(rows, gram_ref, mel):
    weighted = mm(gram_ref[0:256], rows) + mm(gram_ref[256:512], rows)
    rows = rows.astype(F32)
    spread = jnp.sum(weighted * rows, axis=0, keepdims=True)
    inverse = lax.rsqrt(jnp.maximum(spread, 0.0) + EPS)
    latent = (rows[0:mel] + rows[2 * mel : 3 * mel]) * inverse
    high = latent.astype(BF16)
    which = lax.broadcasted_iota(jnp.int32, (256 - 3 * mel, rows.shape[1]), 0)
    return jnp.concatenate(
        [
            high,
            (rows[mel : 2 * mel] * inverse).astype(BF16),
            (latent - high.astype(F32)).astype(BF16),
            jnp.where(which < 2, 1.0, 0.0).astype(BF16),
        ],
        axis=0,
    )


def split_values(values, start, value_ref):
    left = lax.broadcasted_iota(jnp.int32, (values.shape[0], 128), 1) < 64
    for part in range(2):
        pair = values[:, 128 * part : 128 * (part + 1)]
        at = 2 * start + 256 * part
        value_ref[:, at : at + 128] = jnp.where(left, pair, 0.0).astype(BF16)
        value_ref[:, at + 128 : at + 256] = jnp.where(left, 0.0, pair).astype(BF16)


def pair_queries(query, tile):
    row = lax.broadcasted_iota(jnp.int32, (TILE, 128), 0)
    lane = lax.broadcasted_iota(jnp.int32, (TILE, 128), 1)
    chosen = (lane == tile * (TILE // BLK) + row // BLK).astype(F32).astype(BF16)
    return jnp.concatenate([query, chosen], axis=1)


def pair_scores(queries, key_left, key_right, bias):
    gap = jnp.zeros_like(key_left)
    key = jnp.concatenate(
        [
            jnp.concatenate([key_left, gap, bias], axis=0),
            jnp.concatenate([gap, key_right, bias], axis=0),
        ],
        axis=1,
    )
    return mm(queries, key)


def pair_sums(scores, value_left, value_right):
    left = lax.broadcasted_iota(jnp.int32, value_left.shape, 1) < 64
    ones_left = jnp.where(left, 1.0, 0.0).astype(BF16)
    ones_right = jnp.where(left, 0.0, 1.0).astype(BF16)
    value = jnp.concatenate(
        [
            jnp.concatenate([value_left, ones_left], axis=1),
            jnp.concatenate([value_right, ones_right], axis=1),
        ],
        axis=0,
    )
    return mm(jnp.exp2(scores).astype(BF16), value)


def less_top(scores, tops):
    size = scores.shape[1] // 2
    return jnp.concatenate([scores[:, :size] - tops[0], scores[:, size:] - tops[1]], axis=1)


def top_of(scores):
    size = scores.shape[1] // 2
    return (
        jnp.max(scores[:, :size], axis=-1, keepdims=True),
        jnp.max(scores[:, size:], axis=-1, keepdims=True),
    )


def in_range(least, most):
    return (jnp.min(least) > SMALL) & (jnp.max(most) < LARGE)


def pair_keys(key_ref, pair, window):
    return (
        key_ref[pl.ds(pair * 128, 64), window],
        key_ref[pl.ds(pair * 128 + 64, 64), window],
    )


def pair_values(value_ref, pair, window):
    return (
        value_ref[window, pl.ds(pair * 256, 128)],
        value_ref[window, pl.ds(pair * 256 + 128, 128)],
    )


def edges_of(frames):
    own = TILE + HALO
    return (
        (0, 0, 0, HALO, 0),
        (frames // TILE - 1, frames - own, HALO, frames + HALO - own, frames + HALO),
    )


def layer_kernel(
    mel,
    share_ref,
    own_ref,
    mixed_ref,
    keyed_ref,
    gram_ref,
    bias_ref,
    embed_ref,
    gate_ref,
    out_w_ref,
    latent_ref,
    query_ref,
    key_ref,
    value_ref,
    done_ref,
    first_ref,
    sums_ref,
    totals_ref,
    context_ref,
    sems,
):
    share = pltpu.make_async_copy(share_ref, latent_ref, sems.at[0])
    share.start()
    frames, width = query_ref.shape
    pairs = width // 128
    own = own_ref[...]
    normed = normalised(own, gram_ref, mel)
    turned = normed.T
    for start in range(0, width, 256):
        cols = slice(start, start + 256)
        key_ref[cols] = mm(keyed_ref[cols], normed).astype(BF16)
        query_ref[:, cols] = mm(turned, mixed_ref[:, cols]).astype(BF16)
        split_values(
            mm(turned, mixed_ref[:, width + start : width + start + 256]), start, value_ref
        )

    def attend(tile, pair, stable):
        at = tile * TILE
        cols = pl.ds(pair * 128, 128)
        window = pl.ds(at - HALO, TILE + 2 * HALO)
        queries = pair_queries(query_ref[pl.ds(at, TILE), cols], tile)
        scores = pair_scores(
            queries, *pair_keys(key_ref, pair, window), bias_ref[:, pl.ds(at, TILE + 2 * HALO)]
        )
        if stable:
            scores = less_top(scores, top_of(scores))
        sums = pair_sums(scores, *pair_values(value_ref, pair, window))
        total = sums[:, 128:]
        context_ref[pl.ds(at - HALO, TILE), cols] = (sums[:, :128] / total).astype(BF16)
        return total

    first, last = HALO // TILE, (frames - HALO) // TILE
    least = jnp.full((TILE, 128), 1.0, F32)
    most = jnp.full((TILE, 128), 1.0, F32)
    for tile in range(first, last):
        for pair in range(pairs):
            total = attend(tile, pair, False)
            least = jnp.minimum(least, total)
            most = jnp.maximum(most, total)
    for edge, (tile, at, _, bias_at, _) in enumerate(edges_of(frames)):
        window = pl.ds(at, TILE + HALO)
        here = slice(edge * TILE, (edge + 1) * TILE)
        for pair in range(pairs):
            cols = slice(pair * 128, (pair + 1) * 128)
            queries = pair_queries(query_ref[tile * TILE : (tile + 1) * TILE, cols], tile)
            scores = pair_scores(
                queries,
                *pair_keys(key_ref, pair, window),
                bias_ref[:, bias_at : bias_at + TILE + HALO],
            )
            sums = pair_sums(scores, *pair_values(value_ref, pair, window))
            sums_ref[here, cols] = sums[:, :128]
            totals_ref[here, cols] = sums[:, 128:]

    def project():
        own_turned = own_ref[...].T
        for start in range(0, width, 512):
            cols = slice(start, start + 512)
            start_rows = mm(own_turned, embed_ref[:, cols])
            projected = mm(context_ref[...], out_w_ref[:, cols])
            done_ref[:, cols] = (
                start_rows[HALO : frames - HALO] + gate_ref[:, cols] * projected
            ).astype(BF16)
            first_ref[0:HALO, cols] = start_rows[0:HALO]
            first_ref[HALO : 2 * HALO, cols] = start_rows[frames - HALO :]

    project()

    @pl.when(jnp.logical_not(in_range(least, most)))
    def _():
        def one(index, carry):
            attend(first + index // pairs, index % pairs, True)
            return carry

        lax.fori_loop(0, (last - first) * pairs, one, 0)
        project()

    share.wait()


def layer_call(share, own, mixed, keyed, gram, bias, embed, gate, out_w):
    mel, frames = share.shape[0], own.shape[1]
    width = out_w.shape[0]
    return pl.pallas_call(
        functools.partial(layer_kernel, mel),
        in_specs=[whole()] * 9,
        out_specs=[whole(pltpu.HBM)] + [whole()] * 7,
        out_shape=[
            jax.ShapeDtypeStruct(share.shape, F32),
            jax.ShapeDtypeStruct((frames, width), BF16),
            jax.ShapeDtypeStruct((width, frames), BF16),
            jax.ShapeDtypeStruct((frames, 2 * width), BF16),
            jax.ShapeDtypeStruct((frames - 2 * HALO, width), BF16),
            jax.ShapeDtypeStruct((2 * HALO, width), F32),
            jax.ShapeDtypeStruct((2 * TILE, width), F32),
            jax.ShapeDtypeStruct((2 * TILE, width), F32),
        ],
        scratch_shapes=[
            pltpu.VMEM((frames - 2 * HALO, width), BF16),
            pltpu.SemaphoreType.DMA((1,)),
        ],
        compiler_params=pltpu.CompilerParams(vmem_limit_bytes=VMEM_LIMIT),
        cost_estimate=pl.CostEstimate(
            flops=5_000_000_000, bytes_accessed=6_000_000, transcendentals=2_000_000
        ),
        name="layer",
    )(share, own, mixed, keyed, gram, bias, embed, gate, out_w)


def close_kernel(
    far_ref,
    cross_ref,
    prompt_ref,
    mixed_ref,
    keyed_ref,
    gram_ref,
    bias_ref,
    query_ref,
    key_ref,
    value_ref,
    sums_ref,
    totals_ref,
    first_ref,
    gate_ref,
    out_w_ref,
    done_ref,
    next_ref,
    near_key_ref,
    near_value_ref,
    context_ref,
    edge_ref,
    sems,
):
    half, branch, _ = location()
    frames, width = query_ref.shape
    pairs = width // 128
    mel = cross_ref.shape[0]
    inner = pltpu.make_async_copy(done_ref, next_ref.at[pl.ds(HALO, frames - 2 * HALO)], sems.at[0])
    inner.start()
    flag = jnp.where(branch == 0, 1.0, 0.0)
    prompt = jnp.where(
        half == 0, prompt_ref[:, frames : frames + HALO], prompt_ref[:, frames - HALO : frames]
    )
    blank = jnp.zeros((256 - 2 * mel, HALO), F32)
    far = far_ref[...].astype(F32)
    cross_rows = jnp.concatenate([cross_ref[...].astype(F32), prompt * flag, blank], axis=0)
    seq_rows = jnp.concatenate([far[0:mel], far[mel:] * flag, blank], axis=0)
    before = jnp.where(half == 0, seq_rows, cross_rows).astype(BF16)
    after = jnp.where(half == 0, cross_rows, seq_rows).astype(BF16)
    normed = normalised(jnp.concatenate([before, after], axis=1), gram_ref, mel)
    turned = normed.T
    for start in range(0, width, 256):
        cols = slice(start, start + 256)
        near_key_ref[cols] = mm(keyed_ref[cols], normed).astype(BF16)
        split_values(
            mm(turned, mixed_ref[:, width + start : width + start + 256]), start, near_value_ref
        )

    edges = edges_of(frames)
    least = jnp.full((TILE, 128), 1.0, F32)
    most = jnp.full((TILE, 128), 1.0, F32)
    for edge, (tile, _, near_at, _, bias_at) in enumerate(edges):
        window = pl.ds(near_at, HALO)
        here = slice(edge * TILE, (edge + 1) * TILE)
        for pair in range(pairs):
            cols = slice(pair * 128, (pair + 1) * 128)
            queries = pair_queries(query_ref[tile * TILE : (tile + 1) * TILE, cols], tile)
            scores = pair_scores(
                queries,
                *pair_keys(near_key_ref, pair, window),
                bias_ref[:, bias_at : bias_at + HALO],
            )
            sums = pair_sums(scores, *pair_values(near_value_ref, pair, window))
            total = sums[:, 128:] + totals_ref[here, cols]
            context_ref[here, cols] = ((sums[:, :128] + sums_ref[here, cols]) / total).astype(BF16)
            least = jnp.minimum(least, total)
            most = jnp.maximum(most, total)

    columns = 256
    copies = []
    for start in range(0, width, columns):
        for edge, row in enumerate((0, frames - HALO)):
            cols = pl.ds(start, columns)
            copies.append(
                pltpu.make_async_copy(
                    edge_ref.at[pl.ds(edge * HALO, HALO), cols],
                    next_ref.at[pl.ds(row, HALO), cols],
                    sems.at[1 + len(copies)],
                )
            )

    def finish():
        for index, start in enumerate(range(0, width, columns)):
            cols = slice(start, start + columns)
            projected = mm(context_ref[...], out_w_ref[:, cols])
            edge_ref[:, cols] = (first_ref[:, cols] + gate_ref[:, cols] * projected).astype(BF16)
            copies[2 * index].start()
            copies[2 * index + 1].start()

    def settle():
        for copy in copies:
            copy.wait()

    finish()

    @pl.when(jnp.logical_not(in_range(least, most)))
    def _():
        settle()
        for edge, (tile, at, near_at, bias_own, bias_near) in enumerate(edges):
            here = slice(edge * TILE, (edge + 1) * TILE)

            def one(pair, carry):
                cols = pl.ds(pair * 128, 128)
                own_window = pl.ds(at, TILE + HALO)
                near_window = pl.ds(near_at, HALO)
                queries = pair_queries(query_ref[tile * TILE : (tile + 1) * TILE, cols], tile)
                own_scores = pair_scores(
                    queries,
                    *pair_keys(key_ref, pair, own_window),
                    bias_ref[:, bias_own : bias_own + TILE + HALO],
                )
                near_scores = pair_scores(
                    queries,
                    *pair_keys(near_key_ref, pair, near_window),
                    bias_ref[:, bias_near : bias_near + HALO],
                )
                tops = [
                    jnp.maximum(a, b) for a, b in zip(top_of(own_scores), top_of(near_scores))
                ]
                sums = pair_sums(
                    less_top(own_scores, tops), *pair_values(value_ref, pair, own_window)
                ) + pair_sums(
                    less_top(near_scores, tops), *pair_values(near_value_ref, pair, near_window)
                )
                context_ref[here, cols] = (sums[:, :128] / sums[:, 128:]).astype(BF16)
                return carry

            lax.fori_loop(0, pairs, one, 0)

        finish()

    inner.wait()
    settle()


def close_call(
    far, cross, prompt, mixed, keyed, gram, bias, query, key, value, sums, totals, first, gate, out_w, done
):
    frames, width = query.shape
    return pl.pallas_call(
        close_kernel,
        in_specs=[whole()] * 16,
        out_specs=whole(pltpu.HBM),
        out_shape=jax.ShapeDtypeStruct((frames, width), BF16),
        scratch_shapes=[
            pltpu.VMEM((width, 2 * HALO), BF16),
            pltpu.VMEM((2 * HALO, 2 * width), BF16),
            pltpu.VMEM((2 * TILE, width), BF16),
            pltpu.VMEM((2 * TILE, width), BF16),
            pltpu.SemaphoreType.DMA((9,)),
        ],
        compiler_params=pltpu.CompilerParams(vmem_limit_bytes=VMEM_LIMIT),
        cost_estimate=pl.CostEstimate(
            flops=2_000_000_000, bytes_accessed=6_000_000, transcendentals=1_000_000
        ),
        name="close",
    )(
        far,
        cross,
        prompt,
        mixed,
        keyed,
        gram,
        bias,
        query,
        key,
        value,
        sums,
        totals,
        first,
        gate,
        out_w,
        done,
    )


def body(
    hidden,
    latent,
    prompt_mel,
    window_back,
    window_ahead,
    step_index,
    proj_weight,
    latent_weight,
    prompt_weight,
    time_weight,
    qkv_weight,
    attn_out_weight,
):
    axes = ("seq", "cfg")
    spans = lax.axis_size("seq")
    total_blocks = 2 * spans * (hidden.shape[0] // BLK)

    def at(span, cell):
        return span * 4 + cell

    everyone = [(span, cell) for span in range(spans) for cell in range(4)]
    to_partner = [(at(s, c), at(s, c ^ 1)) for s, c in everyone]
    to_half = [(at(s, c), at(s, c ^ 3)) for s, c in everyone]
    to_span = [
        (at(s, c), at(s + (1 if c >= 2 else -1), c ^ 3))
        for s, c in everyone
        if 0 <= s + (1 if c >= 2 else -1) < spans
    ]
    vel, sent = velocity_call(hidden, proj_weight.T)
    sent, step_index = lax.optimization_barrier((sent, step_index))
    partner = lax.ppermute(sent, axes, to_partner)
    mixed, keyed, gram, embed, gate, bias, delta = prepare_call(
        total_blocks,
        step_index,
        window_back,
        window_ahead,
        latent_weight,
        prompt_weight,
        time_weight,
        qkv_weight,
    )
    far = far_call(delta, vel, partner, latent, prompt_mel)
    far = lax.ppermute(far, axes, to_span)
    share, own, cross = combine_call(delta, vel, partner, latent, prompt_mel)
    cross = lax.ppermute(cross, axes, to_half)
    latent_out, query, key, value, done, first, sums, totals = layer_call(
        share, own, mixed, keyed, gram, bias, embed, gate, attn_out_weight
    )
    hidden_next = close_call(
        far,
        cross,
        prompt_mel,
        mixed,
        keyed,
        gram,
        bias,
        query,
        key,
        value,
        sums,
        totals,
        first,
        gate,
        attn_out_weight,
        done,
    )
    return (latent_out, hidden_next)


def solution(mesh):
    in_specs = (
        P(("seq", "cfg"), None),
        P(None, "seq"),
        P(None, "seq"),
        P("seq"),
        P("seq"),
        P(),
        P(),
        P(),
        P(),
        P(),
        P(),
        P(),
    )
    out_specs = (P(None, ("seq", "cfg")), P(("seq", "cfg"), None))
    return jax.shard_map(body, mesh=mesh, in_specs=in_specs, out_specs=out_specs, check_vma=False)
```

```python
import functools
import math

import jax
import jax.numpy as jnp
from jax import lax
from jax.experimental import pallas as pl
from jax.experimental.pallas import tpu as pltpu
from jax.sharding import PartitionSpec as P

HEADS = 16
BLK = 32
NSTEPS = 32
HALO = 128
EPS = 1e-06
GUIDE = 0.5
TILE = 128
MASKED = -1e30
SMALL = 1e-30
LARGE = 1e30

F32 = jnp.float32
BF16 = jnp.bfloat16
VMEM_LIMIT = 24 * 1024 * 1024
SMALL_VMEM = 8 * 1024 * 1024


def mm(a, b):
    return jnp.dot(a, b, preferred_element_type=F32)


def mm_nt(a, b):
    return lax.dot_general(a, b, (((1,), (1,)), ((), ())), preferred_element_type=F32)


def whole(memory_space=pltpu.VMEM):
    return pl.BlockSpec(memory_space=memory_space)


def in_hbm(array):
    return pltpu.with_memory_space_constraint(array, pltpu.HBM)


def location():
    place = lax.axis_index("cfg")
    half = place // 2
    return half, place % 2, 2 * lax.axis_index("seq") + half


def sin_cos(angle):
    turns = jnp.floor(angle * (2.0 / math.pi) + 0.5)
    rest = angle - turns * 1.5703125
    rest = rest - turns * 4.837512969970703125e-4
    rest = rest - turns * 7.549789954891882e-8
    square = rest * rest
    sine = rest + rest * square * (
        -1.6666654611e-1 + square * (8.3321608736e-3 - square * 1.9515295891e-4)
    )
    cosine = (
        1.0
        - 0.5 * square
        + square
        * square
        * (4.166664568298827e-2 + square * (-1.388731625493765e-3 + square * 2.443315711809948e-5))
    )
    quarter = turns - 4.0 * jnp.floor(turns * 0.25)
    odd = (quarter == 1.0) | (quarter == 3.0)
    sine, cosine = jnp.where(odd, cosine, sine), jnp.where(odd, sine, cosine)
    sine = jnp.where(quarter >= 2.0, -sine, sine)
    cosine = jnp.where((quarter == 1.0) | (quarter == 2.0), -cosine, cosine)
    return sine, cosine


def time_value(step):
    return 1.0 - sin_cos(0.5 * math.pi * step / NSTEPS)[1]


def time_features(step):
    later = time_value(step + 1.0)
    half_freq = step.shape[1] // 2
    lane = lax.broadcasted_iota(jnp.int32, step.shape, 1)
    which = jnp.where(lane < half_freq, lane, lane - half_freq).astype(F32)
    freqs = jnp.exp(-math.log(10000.0) * which / half_freq)
    sine, cosine = sin_cos(1000.0 * later * freqs)
    return jnp.where(lane < half_freq, sine, cosine)


def velocity_kernel(hidden_ref, weight_ref, vel_ref, sent_ref, rows_ref, held_ref, sems):
    parts = sems.shape[0] - 1
    size = hidden_ref.shape[0] // parts
    copies = []
    for part in range(parts):
        here = pl.ds(part * size, size)
        copies.append(
            pltpu.make_async_copy(hidden_ref.at[here], rows_ref.at[here], sems.at[part])
        )
    copies.append(pltpu.make_async_copy(weight_ref, held_ref, sems.at[parts]))
    for copy in reversed(copies):
        copy.start()
    copies[parts].wait()
    weight = held_ref[...]
    for copy in copies[:parts]:
        copy.wait()
    for part in range(parts):
        here = slice(part * size, (part + 1) * size)
        rows = rows_ref[here].astype(F32)
        mean = jnp.mean(rows, axis=-1, keepdims=True)
        centered = rows - mean
        spread = jnp.mean(centered * centered, axis=-1, keepdims=True)
        normed = (centered * lax.rsqrt(spread + EPS)).astype(BF16)
        vel = mm_nt(weight, normed)
        vel_ref[:, here] = vel
        sent_ref[:, here] = vel.astype(BF16)


def velocity_call(hidden, proj_turned):
    rows, width = hidden.shape
    mel = proj_turned.shape[0]
    return pl.pallas_call(
        velocity_kernel,
        in_specs=[whole(pltpu.HBM)] * 2,
        out_specs=[whole()] * 2,
        out_shape=[
            jax.ShapeDtypeStruct((mel, rows), F32),
            jax.ShapeDtypeStruct((mel, rows), BF16),
        ],
        scratch_shapes=[
            pltpu.VMEM((rows, width), BF16),
            pltpu.VMEM((mel, width), BF16),
            pltpu.SemaphoreType.DMA((5,)),
        ],
        compiler_params=pltpu.CompilerParams(vmem_limit_bytes=SMALL_VMEM),
        cost_estimate=pl.CostEstimate(
            flops=10_000_000_000, bytes_accessed=2 * rows * width, transcendentals=0
        ),
        name="velocity",
    )(in_hbm(hidden), in_hbm(proj_turned))


def prepare_kernel(
    total_blocks,
    step_ref,
    back_hbm,
    ahead_hbm,
    latent_w_hbm,
    prompt_w_hbm,
    time_w_ref,
    qkv_ref,
    mixed_ref,
    keyed_ref,
    gram_ref,
    embed_ref,
    gate_ref,
    bias_ref,
    delta_ref,
    left_ref,
    back_ref,
    ahead_ref,
    latent_w_ref,
    prompt_w_ref,
    sems,
):
    mel, width = latent_w_ref.shape
    small = [
        pltpu.make_async_copy(source, target, sems.at[index])
        for index, (source, target) in enumerate(
            [
                (latent_w_hbm, latent_w_ref),
                (prompt_w_hbm, prompt_w_ref),
                (back_hbm, back_ref),
                (ahead_hbm, ahead_ref),
            ]
        )
    ]
    parts = 3
    columns = 3 * width // parts
    for copy in small:
        copy.start()

    small[0].wait()
    small[1].wait()
    both = jnp.concatenate([latent_w_ref[...], prompt_w_ref[...]], axis=0)
    wide = both.astype(F32)
    centered = wide - jnp.mean(wide, axis=-1, keepdims=True)
    embed = jnp.concatenate(
        [both, latent_w_ref[...], jnp.zeros((256 - 3 * mel, width), BF16)], axis=0
    )
    embed_ref[...] = embed
    col = jnp.mean(embed.astype(F32), axis=-1, keepdims=True)
    row = mm_nt(jnp.ones((16, width), BF16), embed)[0:1] / width
    gram = mm_nt(embed, embed) / width - col * row
    gram_high = gram.astype(BF16)
    gram_ref[0:256] = gram_high
    gram_ref[256:512] = (gram - gram_high.astype(F32)).astype(BF16)

    step = jnp.full((1, time_w_ref.shape[0]), step_ref[0], jnp.int32).astype(F32)
    feats = jnp.broadcast_to(time_features(step), (16, step.shape[1]))
    step = step[:, :128]
    delta_ref[...] = time_value(step + 1.0) - time_value(step)
    high = feats.astype(BF16)
    rest = feats - high.astype(F32)
    mid = rest.astype(BF16)
    low = (rest - mid.astype(F32)).astype(BF16)
    pieces = mm(jnp.concatenate([high, mid, low], axis=0), time_w_ref[...])
    mod = pieces[0:1] + (pieces[16:17] + pieces[32:33])
    shift, scale, gate = mod[:, :width], mod[:, width : 2 * width], mod[:, 2 * width :]
    gate_ref[...] = gate
    left_ref[0 : 2 * mel] = (centered * (1.0 + scale)).astype(BF16)
    shift_high = shift.astype(BF16).astype(F32)
    which = lax.broadcasted_iota(jnp.int32, (16, width), 0)
    left_ref[2 * mel : 2 * mel + 16] = jnp.where(
        which == 0, shift_high, jnp.where(which == 1, shift - shift_high, 0.0)
    ).astype(BF16)

    small[2].wait()
    small[3].wait()
    half, _, span = location()
    per_half = back_ref.shape[0] // 2
    keys = bias_ref.shape[1]
    row_block = lax.broadcasted_iota(jnp.int32, (16, keys), 0)
    lower = jnp.zeros((16, keys), jnp.int32)
    upper = jnp.zeros((16, keys), jnp.int32)
    for block in range(per_half):
        lower = jnp.where(row_block == block, block - back_ref[half * per_half + block], lower)
        upper = jnp.where(row_block == block, block + ahead_ref[half * per_half + block], upper)
    key_block = lax.broadcasted_iota(jnp.int32, (16, keys), 1) // BLK - HALO // BLK
    place = key_block + span * per_half
    seen = (key_block >= lower) & (key_block <= upper) & (place >= 0) & (place < total_blocks)
    bias_ref[0:16] = jnp.where(seen, 0.0, MASKED).astype(BF16)
    bias_ref[16:128] = jnp.zeros((112, keys), BF16)

    left = left_ref[...]
    for part in range(parts):
        start = part * columns
        acc = mm(left, qkv_ref[:, start : start + columns])
        if start < width:
            acc = acc * (math.log2(math.e) / math.sqrt(width // HEADS))
        offset = acc[2 * mel : 2 * mel + 1] + acc[2 * mel + 1 : 2 * mel + 2]
        offset_high = offset.astype(BF16).astype(F32)
        which = lax.broadcasted_iota(jnp.int32, (256 - 3 * mel, columns), 0)
        last = jnp.where(which == 0, offset_high, jnp.where(which == 1, offset - offset_high, 0.0))
        block = jnp.concatenate([acc[: 2 * mel], acc[:mel], last], axis=0).astype(BF16)
        if start < width:
            mixed_ref[:, start : start + columns] = block
        elif start < 2 * width:
            keyed_ref[start - width : start - width + columns] = block.T
        else:
            mixed_ref[:, start - width : start - width + columns] = block


def prepare_call(
    total_blocks, step_index, back, ahead, latent_weight, prompt_weight, time_weight, qkv_weight
):
    mel, width = latent_weight.shape
    return pl.pallas_call(
        functools.partial(prepare_kernel, total_blocks),
        in_specs=[whole(pltpu.SMEM)] + [whole(pltpu.HBM)] * 4 + [whole()] * 2,
        out_specs=[whole()] * 7,
        out_shape=[
            jax.ShapeDtypeStruct((256, 2 * width), BF16),
            jax.ShapeDtypeStruct((width, 256), BF16),
            jax.ShapeDtypeStruct((512, 256), BF16),
            jax.ShapeDtypeStruct((256, width), BF16),
            jax.ShapeDtypeStruct((1, width), F32),
            jax.ShapeDtypeStruct((128, 512 + 2 * HALO), BF16),
            jax.ShapeDtypeStruct((1, 128), F32),
        ],
        scratch_shapes=[
            pltpu.VMEM((2 * mel + 16, width), BF16),
            pltpu.SMEM(back.shape, jnp.int32),
            pltpu.SMEM(ahead.shape, jnp.int32),
            pltpu.VMEM(latent_weight.shape, BF16),
            pltpu.VMEM(prompt_weight.shape, BF16),
            pltpu.SemaphoreType.DMA((4,)),
        ],
        compiler_params=pltpu.CompilerParams(vmem_limit_bytes=VMEM_LIMIT),
        cost_estimate=pl.CostEstimate(
            flops=2 * 256 * width * 3 * width, bytes_accessed=8 * width * width, transcendentals=0
        ),
        name="prepare",
    )(
        step_index,
        in_hbm(back),
        in_hbm(ahead),
        in_hbm(latent_weight),
        in_hbm(prompt_weight),
        time_weight,
        qkv_weight,
    )


def weights_of(delta_ref):
    branch = lax.axis_index("cfg") % 2
    delta = delta_ref[0:1, 0:1]
    mine = jnp.where(branch == 0, 1.0 + GUIDE, -GUIDE) * delta
    other = jnp.where(branch == 0, -GUIDE, 1.0 + GUIDE) * delta
    return mine, other


def updated_end(refs, half, own, whole_block):
    delta_ref, vel_ref, partner_ref, latent_ref = refs

    def ends(ref, places):
        head, tail = places
        return jnp.where(half == 0, ref[:, head : head + HALO], ref[:, tail : tail + HALO])

    mine, other = weights_of(delta_ref)
    return (
        ends(latent_ref, whole_block)
        + (mine * ends(vel_ref, own) + other * ends(partner_ref, own).astype(F32))
    ).astype(BF16)


def far_kernel(delta_ref, vel_ref, partner_ref, latent_ref, prompt_ref, far_ref):
    half, _, _ = location()
    mel, frames = vel_ref.shape
    last = 2 * frames - HALO
    far_ref[0:mel] = updated_end(
        (delta_ref, vel_ref, partner_ref, latent_ref), half, (0, frames - HALO), (0, last)
    )
    far_ref[mel : 2 * mel] = jnp.where(
        half == 0, prompt_ref[:, :HALO], prompt_ref[:, last:]
    ).astype(BF16)


def combine_kernel(
    delta_ref, vel_ref, partner_ref, latent_ref, prompt_ref, next_ref, rows_ref, cross_ref
):
    half, branch, _ = location()
    mel, frames = vel_ref.shape
    mine, other = weights_of(delta_ref)
    latent = jnp.where(half == 0, latent_ref[:, :frames], latent_ref[:, frames:])
    prompt = jnp.where(half == 0, prompt_ref[:, :frames], prompt_ref[:, frames:])
    updated = latent + (mine * vel_ref[...] + other * partner_ref[...].astype(F32))
    head, tail = updated[:, :HALO], updated[:, frames - HALO :]
    cross_ref[...] = jnp.where(half == 0, tail, head).astype(BF16)
    share = frames // 2
    next_ref[...] = jnp.where(branch == 0, updated[:, :share], updated[:, share:])
    high = updated.astype(BF16)
    rows_ref[0:mel] = high
    rows_ref[mel : 2 * mel] = jnp.where(branch == 0, prompt, 0.0).astype(BF16)
    rows_ref[2 * mel : 3 * mel] = (updated - high.astype(F32)).astype(BF16)
    rows_ref[3 * mel : 256] = jnp.zeros((256 - 3 * mel, frames), BF16)


def combine_call(delta, vel, partner, latent, prompt):
    mel, frames = vel.shape
    return pl.pallas_call(
        combine_kernel,
        in_specs=[whole()] * 5,
        out_specs=[whole()] * 3,
        out_shape=[
            jax.ShapeDtypeStruct((mel, frames // 2), F32),
            jax.ShapeDtypeStruct((256, frames), BF16),
            jax.ShapeDtypeStruct((mel, HALO), BF16),
        ],
        compiler_params=pltpu.CompilerParams(vmem_limit_bytes=SMALL_VMEM),
        cost_estimate=pl.CostEstimate(
            flops=5_000_000_000, bytes_accessed=1_000_000, transcendentals=0
        ),
        name="combine",
    )(delta, vel, partner, latent, prompt)


def far_call(delta, vel, partner, latent, prompt):
    return pl.pallas_call(
        far_kernel,
        in_specs=[whole()] * 5,
        out_specs=whole(),
        out_shape=jax.ShapeDtypeStruct((2 * vel.shape[0], HALO), BF16),
        compiler_params=pltpu.CompilerParams(vmem_limit_bytes=SMALL_VMEM),
        name="far",
    )(delta, vel, partner, latent, prompt)


def normalised(rows, gram_ref, mel):
    weighted = mm(gram_ref[0:256], rows) + mm(gram_ref[256:512], rows)
    rows = rows.astype(F32)
    spread = jnp.sum(weighted * rows, axis=0, keepdims=True)
    inverse = lax.rsqrt(jnp.maximum(spread, 0.0) + EPS)
    latent = (rows[0:mel] + rows[2 * mel : 3 * mel]) * inverse
    high = latent.astype(BF16)
    which = lax.broadcasted_iota(jnp.int32, (256 - 3 * mel, rows.shape[1]), 0)
    return jnp.concatenate(
        [
            high,
            (rows[mel : 2 * mel] * inverse).astype(BF16),
            (latent - high.astype(F32)).astype(BF16),
            jnp.where(which < 2, 1.0, 0.0).astype(BF16),
        ],
        axis=0,
    )


def split_values(values, start, value_ref):
    left = lax.broadcasted_iota(jnp.int32, (values.shape[0], 128), 1) < 64
    for part in range(2):
        pair = values[:, 128 * part : 128 * (part + 1)]
        at = 2 * start + 256 * part
        value_ref[:, at : at + 128] = jnp.where(left, pair, 0.0).astype(BF16)
        value_ref[:, at + 128 : at + 256] = jnp.where(left, 0.0, pair).astype(BF16)


def pair_queries(query, tile):
    row = lax.broadcasted_iota(jnp.int32, (TILE, 128), 0)
    lane = lax.broadcasted_iota(jnp.int32, (TILE, 128), 1)
    chosen = (lane == tile * (TILE // BLK) + row // BLK).astype(F32).astype(BF16)
    return jnp.concatenate([query, chosen], axis=1)


def pair_scores(queries, key_left, key_right, bias):
    gap = jnp.zeros_like(key_left)
    key = jnp.concatenate(
        [
            jnp.concatenate([key_left, gap, bias], axis=0),
            jnp.concatenate([gap, key_right, bias], axis=0),
        ],
        axis=1,
    )
    return mm(queries, key)


def pair_sums(scores, value_left, value_right):
    left = lax.broadcasted_iota(jnp.int32, value_left.shape, 1) < 64
    ones_left = jnp.where(left, 1.0, 0.0).astype(BF16)
    ones_right = jnp.where(left, 0.0, 1.0).astype(BF16)
    value = jnp.concatenate(
        [
            jnp.concatenate([value_left, ones_left], axis=1),
            jnp.concatenate([value_right, ones_right], axis=1),
        ],
        axis=0,
    )
    return mm(jnp.exp2(scores).astype(BF16), value)


def less_top(scores, tops):
    size = scores.shape[1] // 2
    return jnp.concatenate([scores[:, :size] - tops[0], scores[:, size:] - tops[1]], axis=1)


def top_of(scores):
    size = scores.shape[1] // 2
    return (
        jnp.max(scores[:, :size], axis=-1, keepdims=True),
        jnp.max(scores[:, size:], axis=-1, keepdims=True),
    )


def in_range(least, most):
    return (jnp.min(least) > SMALL) & (jnp.max(most) < LARGE)


def pair_keys(key_ref, pair, window):
    return (
        key_ref[pl.ds(pair * 128, 64), window],
        key_ref[pl.ds(pair * 128 + 64, 64), window],
    )


def pair_values(value_ref, pair, window):
    return (
        value_ref[window, pl.ds(pair * 256, 128)],
        value_ref[window, pl.ds(pair * 256 + 128, 128)],
    )


def edges_of(frames):
    own = TILE + HALO
    return (
        (0, 0, 0, HALO, 0),
        (frames // TILE - 1, frames - own, HALO, frames + HALO - own, frames + HALO),
    )


def layer_kernel(
    mel,
    share_ref,
    own_ref,
    mixed_ref,
    keyed_ref,
    gram_ref,
    bias_ref,
    embed_ref,
    gate_ref,
    out_w_ref,
    latent_ref,
    query_ref,
    key_ref,
    value_ref,
    done_ref,
    first_ref,
    sums_ref,
    totals_ref,
    context_ref,
    sems,
):
    share = pltpu.make_async_copy(share_ref, latent_ref, sems.at[0])
    share.start()
    frames, width = query_ref.shape
    pairs = width // 128
    own = own_ref[...]
    normed = normalised(own, gram_ref, mel)
    turned = normed.T
    for start in range(0, width, 256):
        cols = slice(start, start + 256)
        key_ref[cols] = mm(keyed_ref[cols], normed).astype(BF16)
        query_ref[:, cols] = mm(turned, mixed_ref[:, cols]).astype(BF16)
        split_values(
            mm(turned, mixed_ref[:, width + start : width + start + 256]), start, value_ref
        )

    def attend(tile, pair, stable):
        at = tile * TILE
        cols = pl.ds(pair * 128, 128)
        window = pl.ds(at - HALO, TILE + 2 * HALO)
        queries = pair_queries(query_ref[pl.ds(at, TILE), cols], tile)
        scores = pair_scores(
            queries, *pair_keys(key_ref, pair, window), bias_ref[:, pl.ds(at, TILE + 2 * HALO)]
        )
        if stable:
            scores = less_top(scores, top_of(scores))
        sums = pair_sums(scores, *pair_values(value_ref, pair, window))
        total = sums[:, 128:]
        context_ref[pl.ds(at - HALO, TILE), cols] = (sums[:, :128] / total).astype(BF16)
        return total

    first, last = HALO // TILE, (frames - HALO) // TILE
    least = jnp.full((TILE, 128), 1.0, F32)
    most = jnp.full((TILE, 128), 1.0, F32)
    for tile in range(first, last):
        for pair in range(pairs):
            total = attend(tile, pair, False)
            least = jnp.minimum(least, total)
            most = jnp.maximum(most, total)
    for edge, (tile, at, _, bias_at, _) in enumerate(edges_of(frames)):
        window = pl.ds(at, TILE + HALO)
        here = slice(edge * TILE, (edge + 1) * TILE)
        for pair in range(pairs):
            cols = slice(pair * 128, (pair + 1) * 128)
            queries = pair_queries(query_ref[tile * TILE : (tile + 1) * TILE, cols], tile)
            scores = pair_scores(
                queries,
                *pair_keys(key_ref, pair, window),
                bias_ref[:, bias_at : bias_at + TILE + HALO],
            )
            sums = pair_sums(scores, *pair_values(value_ref, pair, window))
            sums_ref[here, cols] = sums[:, :128]
            totals_ref[here, cols] = sums[:, 128:]

    def project():
        own_turned = own_ref[...].T
        for start in range(0, width, 512):
            cols = slice(start, start + 512)
            start_rows = mm(own_turned, embed_ref[:, cols])
            projected = mm(context_ref[...], out_w_ref[:, cols])
            done_ref[:, cols] = (
                start_rows[HALO : frames - HALO] + gate_ref[:, cols] * projected
            ).astype(BF16)
            first_ref[0:HALO, cols] = start_rows[0:HALO]
            first_ref[HALO : 2 * HALO, cols] = start_rows[frames - HALO :]

    project()

    @pl.when(jnp.logical_not(in_range(least, most)))
    def _():
        def one(index, carry):
            attend(first + index // pairs, index % pairs, True)
            return carry

        lax.fori_loop(0, (last - first) * pairs, one, 0)
        project()

    share.wait()


def layer_call(share, own, mixed, keyed, gram, bias, embed, gate, out_w):
    mel, frames = share.shape[0], own.shape[1]
    width = out_w.shape[0]
    return pl.pallas_call(
        functools.partial(layer_kernel, mel),
        in_specs=[whole()] * 9,
        out_specs=[whole(pltpu.HBM)] + [whole()] * 7,
        out_shape=[
            jax.ShapeDtypeStruct(share.shape, F32),
            jax.ShapeDtypeStruct((frames, width), BF16),
            jax.ShapeDtypeStruct((width, frames), BF16),
            jax.ShapeDtypeStruct((frames, 2 * width), BF16),
            jax.ShapeDtypeStruct((frames - 2 * HALO, width), BF16),
            jax.ShapeDtypeStruct((2 * HALO, width), F32),
            jax.ShapeDtypeStruct((2 * TILE, width), F32),
            jax.ShapeDtypeStruct((2 * TILE, width), F32),
        ],
        scratch_shapes=[
            pltpu.VMEM((frames - 2 * HALO, width), BF16),
            pltpu.SemaphoreType.DMA((1,)),
        ],
        compiler_params=pltpu.CompilerParams(vmem_limit_bytes=VMEM_LIMIT),
        cost_estimate=pl.CostEstimate(
            flops=5_000_000_000, bytes_accessed=6_000_000, transcendentals=2_000_000
        ),
        name="layer",
    )(share, own, mixed, keyed, gram, bias, embed, gate, out_w)


def close_kernel(
    far_ref,
    cross_ref,
    prompt_ref,
    mixed_ref,
    keyed_ref,
    gram_ref,
    bias_ref,
    query_ref,
    key_ref,
    value_ref,
    sums_ref,
    totals_ref,
    first_ref,
    gate_ref,
    out_w_ref,
    done_ref,
    next_ref,
    near_key_ref,
    near_value_ref,
    context_ref,
    edge_ref,
    sems,
):
    half, branch, _ = location()
    frames, width = query_ref.shape
    pairs = width // 128
    mel = cross_ref.shape[0]
    inner = pltpu.make_async_copy(done_ref, next_ref.at[pl.ds(HALO, frames - 2 * HALO)], sems.at[0])
    inner.start()
    flag = jnp.where(branch == 0, 1.0, 0.0)
    prompt = jnp.where(
        half == 0, prompt_ref[:, frames : frames + HALO], prompt_ref[:, frames - HALO : frames]
    )
    blank = jnp.zeros((256 - 2 * mel, HALO), F32)
    far = far_ref[...].astype(F32)
    cross_rows = jnp.concatenate([cross_ref[...].astype(F32), prompt * flag, blank], axis=0)
    seq_rows = jnp.concatenate([far[0:mel], far[mel:] * flag, blank], axis=0)
    before = jnp.where(half == 0, seq_rows, cross_rows).astype(BF16)
    after = jnp.where(half == 0, cross_rows, seq_rows).astype(BF16)
    normed = normalised(jnp.concatenate([before, after], axis=1), gram_ref, mel)
    turned = normed.T
    for start in range(0, width, 256):
        cols = slice(start, start + 256)
        near_key_ref[cols] = mm(keyed_ref[cols], normed).astype(BF16)
        split_values(
            mm(turned, mixed_ref[:, width + start : width + start + 256]), start, near_value_ref
        )

    edges = edges_of(frames)
    least = jnp.full((TILE, 128), 1.0, F32)
    most = jnp.full((TILE, 128), 1.0, F32)
    for pair in range(pairs):
        cols = slice(pair * 128, (pair + 1) * 128)
        for edge, (tile, _, near_at, _, bias_at) in enumerate(edges):
            window = pl.ds(near_at, HALO)
            here = slice(edge * TILE, (edge + 1) * TILE)
            queries = pair_queries(query_ref[tile * TILE : (tile + 1) * TILE, cols], tile)
            scores = pair_scores(
                queries,
                *pair_keys(near_key_ref, pair, window),
                bias_ref[:, bias_at : bias_at + HALO],
            )
            sums = pair_sums(scores, *pair_values(near_value_ref, pair, window))
            total = sums[:, 128:] + totals_ref[here, cols]
            context_ref[here, cols] = ((sums[:, :128] + sums_ref[here, cols]) / total).astype(BF16)
            least = jnp.minimum(least, total)
            most = jnp.maximum(most, total)

    columns = 256
    copies = []
    for start in range(0, width, columns):
        for edge, row in enumerate((0, frames - HALO)):
            cols = pl.ds(start, columns)
            copies.append(
                pltpu.make_async_copy(
                    edge_ref.at[pl.ds(edge * HALO, HALO), cols],
                    next_ref.at[pl.ds(row, HALO), cols],
                    sems.at[1 + len(copies)],
                )
            )

    def finish():
        for index, start in enumerate(range(0, width, columns)):
            cols = slice(start, start + columns)
            projected = mm(context_ref[...], out_w_ref[:, cols])
            edge_ref[:, cols] = (first_ref[:, cols] + gate_ref[:, cols] * projected).astype(BF16)
            copies[2 * index].start()
            copies[2 * index + 1].start()

    def settle():
        for copy in copies:
            copy.wait()

    finish()

    @pl.when(jnp.logical_not(in_range(least, most)))
    def _():
        settle()
        for edge, (tile, at, near_at, bias_own, bias_near) in enumerate(edges):
            here = slice(edge * TILE, (edge + 1) * TILE)

            def one(pair, carry):
                cols = pl.ds(pair * 128, 128)
                own_window = pl.ds(at, TILE + HALO)
                near_window = pl.ds(near_at, HALO)
                queries = pair_queries(query_ref[tile * TILE : (tile + 1) * TILE, cols], tile)
                own_scores = pair_scores(
                    queries,
                    *pair_keys(key_ref, pair, own_window),
                    bias_ref[:, bias_own : bias_own + TILE + HALO],
                )
                near_scores = pair_scores(
                    queries,
                    *pair_keys(near_key_ref, pair, near_window),
                    bias_ref[:, bias_near : bias_near + HALO],
                )
                tops = [
                    jnp.maximum(a, b) for a, b in zip(top_of(own_scores), top_of(near_scores))
                ]
                sums = pair_sums(
                    less_top(own_scores, tops), *pair_values(value_ref, pair, own_window)
                ) + pair_sums(
                    less_top(near_scores, tops), *pair_values(near_value_ref, pair, near_window)
                )
                context_ref[here, cols] = (sums[:, :128] / sums[:, 128:]).astype(BF16)
                return carry

            lax.fori_loop(0, pairs, one, 0)

        finish()

    inner.wait()
    settle()


def close_call(
    far, cross, prompt, mixed, keyed, gram, bias, query, key, value, sums, totals, first, gate, out_w, done
):
    frames, width = query.shape
    return pl.pallas_call(
        close_kernel,
        in_specs=[whole()] * 16,
        out_specs=whole(pltpu.HBM),
        out_shape=jax.ShapeDtypeStruct((frames, width), BF16),
        scratch_shapes=[
            pltpu.VMEM((width, 2 * HALO), BF16),
            pltpu.VMEM((2 * HALO, 2 * width), BF16),
            pltpu.VMEM((2 * TILE, width), BF16),
            pltpu.VMEM((2 * TILE, width), BF16),
            pltpu.SemaphoreType.DMA((9,)),
        ],
        compiler_params=pltpu.CompilerParams(vmem_limit_bytes=VMEM_LIMIT),
        cost_estimate=pl.CostEstimate(
            flops=2_000_000_000, bytes_accessed=6_000_000, transcendentals=1_000_000
        ),
        name="close",
    )(
        far,
        cross,
        prompt,
        mixed,
        keyed,
        gram,
        bias,
        query,
        key,
        value,
        sums,
        totals,
        first,
        gate,
        out_w,
        done,
    )


def body(
    hidden,
    latent,
    prompt_mel,
    window_back,
    window_ahead,
    step_index,
    proj_weight,
    latent_weight,
    prompt_weight,
    time_weight,
    qkv_weight,
    attn_out_weight,
):
    axes = ("seq", "cfg")
    spans = lax.axis_size("seq")
    total_blocks = 2 * spans * (hidden.shape[0] // BLK)

    def at(span, cell):
        return span * 4 + cell

    everyone = [(span, cell) for span in range(spans) for cell in range(4)]
    to_partner = [(at(s, c), at(s, c ^ 1)) for s, c in everyone]
    to_half = [(at(s, c), at(s, c ^ 3)) for s, c in everyone]
    to_span = [
        (at(s, c), at(s + (1 if c >= 2 else -1), c ^ 3))
        for s, c in everyone
        if 0 <= s + (1 if c >= 2 else -1) < spans
    ]
    vel, sent = velocity_call(hidden, proj_weight.T)
    sent, step_index = lax.optimization_barrier((sent, step_index))
    partner = lax.ppermute(sent, axes, to_partner)
    mixed, keyed, gram, embed, gate, bias, delta = prepare_call(
        total_blocks,
        step_index,
        window_back,
        window_ahead,
        latent_weight,
        prompt_weight,
        time_weight,
        qkv_weight,
    )
    far = far_call(delta, vel, partner, latent, prompt_mel)
    far = lax.ppermute(far, axes, to_span)
    share, own, cross = combine_call(delta, vel, partner, latent, prompt_mel)
    cross = lax.ppermute(cross, axes, to_half)
    latent_out, query, key, value, done, first, sums, totals = layer_call(
        share, own, mixed, keyed, gram, bias, embed, gate, attn_out_weight
    )
    hidden_next = close_call(
        far,
        cross,
        prompt_mel,
        mixed,
        keyed,
        gram,
        bias,
        query,
        key,
        value,
        sums,
        totals,
        first,
        gate,
        attn_out_weight,
        done,
    )
    return (latent_out, hidden_next)


def solution(mesh):
    in_specs = (
        P(("seq", "cfg"), None),
        P(None, "seq"),
        P(None, "seq"),
        P("seq"),
        P("seq"),
        P(),
        P(),
        P(),
        P(),
        P(),
        P(),
        P(),
    )
    out_specs = (P(None, ("seq", "cfg")), P(("seq", "cfg"), None))
    return jax.shard_map(body, mesh=mesh, in_specs=in_specs, out_specs=out_specs, check_vma=False)
```

```python
import functools
import math

import jax
import jax.numpy as jnp
from jax import lax
from jax.experimental import pallas as pl
from jax.experimental.pallas import tpu as pltpu
from jax.sharding import PartitionSpec as P

HEADS = 16
BLK = 32
NSTEPS = 32
HALO = 128
EPS = 1e-06
GUIDE = 0.5
TILE = 128
MASKED = -1e30
SMALL = 1e-30
LARGE = 1e30

F32 = jnp.float32
BF16 = jnp.bfloat16
VMEM_LIMIT = 24 * 1024 * 1024
SMALL_VMEM = 8 * 1024 * 1024


def mm(a, b):
    return jnp.dot(a, b, preferred_element_type=F32)


def mm_nt(a, b):
    return lax.dot_general(a, b, (((1,), (1,)), ((), ())), preferred_element_type=F32)


def whole(memory_space=pltpu.VMEM):
    return pl.BlockSpec(memory_space=memory_space)


def in_hbm(array):
    return pltpu.with_memory_space_constraint(array, pltpu.HBM)


def location():
    place = lax.axis_index("cfg")
    half = place // 2
    return half, place % 2, 2 * lax.axis_index("seq") + half


def sin_cos(angle):
    turns = jnp.floor(angle * (2.0 / math.pi) + 0.5)
    rest = angle - turns * 1.5703125
    rest = rest - turns * 4.837512969970703125e-4
    rest = rest - turns * 7.549789954891882e-8
    square = rest * rest
    sine = rest + rest * square * (
        -1.6666654611e-1 + square * (8.3321608736e-3 - square * 1.9515295891e-4)
    )
    cosine = (
        1.0
        - 0.5 * square
        + square
        * square
        * (4.166664568298827e-2 + square * (-1.388731625493765e-3 + square * 2.443315711809948e-5))
    )
    quarter = turns - 4.0 * jnp.floor(turns * 0.25)
    odd = (quarter == 1.0) | (quarter == 3.0)
    sine, cosine = jnp.where(odd, cosine, sine), jnp.where(odd, sine, cosine)
    sine = jnp.where(quarter >= 2.0, -sine, sine)
    cosine = jnp.where((quarter == 1.0) | (quarter == 2.0), -cosine, cosine)
    return sine, cosine


def time_value(step):
    return 1.0 - sin_cos(0.5 * math.pi * step / NSTEPS)[1]


def time_features(step):
    later = time_value(step + 1.0)
    half_freq = step.shape[1] // 2
    lane = lax.broadcasted_iota(jnp.int32, step.shape, 1)
    which = jnp.where(lane < half_freq, lane, lane - half_freq).astype(F32)
    freqs = jnp.exp(-math.log(10000.0) * which / half_freq)
    sine, cosine = sin_cos(1000.0 * later * freqs)
    return jnp.where(lane < half_freq, sine, cosine)


def velocity_kernel(hidden_ref, weight_ref, vel_ref, sent_ref, rows_ref, held_ref, sems):
    parts = sems.shape[0] - 1
    size = hidden_ref.shape[0] // parts
    copies = []
    for part in range(parts):
        here = pl.ds(part * size, size)
        copies.append(
            pltpu.make_async_copy(hidden_ref.at[here], rows_ref.at[here], sems.at[part])
        )
    copies.append(pltpu.make_async_copy(weight_ref, held_ref, sems.at[parts]))
    for copy in reversed(copies):
        copy.start()
    copies[parts].wait()
    weight = held_ref[...]
    for copy in copies[:parts]:
        copy.wait()
    for part in range(parts):
        here = slice(part * size, (part + 1) * size)
        rows = rows_ref[here].astype(F32)
        mean = jnp.mean(rows, axis=-1, keepdims=True)
        centered = rows - mean
        spread = jnp.mean(centered * centered, axis=-1, keepdims=True)
        normed = (centered * lax.rsqrt(spread + EPS)).astype(BF16)
        vel = mm_nt(weight, normed)
        vel_ref[:, here] = vel
        sent_ref[:, here] = vel.astype(BF16)


def velocity_call(hidden, proj_turned):
    rows, width = hidden.shape
    mel = proj_turned.shape[0]
    return pl.pallas_call(
        velocity_kernel,
        in_specs=[whole(pltpu.HBM)] * 2,
        out_specs=[whole()] * 2,
        out_shape=[
            jax.ShapeDtypeStruct((mel, rows), F32),
            jax.ShapeDtypeStruct((mel, rows), BF16),
        ],
        scratch_shapes=[
            pltpu.VMEM((rows, width), BF16),
            pltpu.VMEM((mel, width), BF16),
            pltpu.SemaphoreType.DMA((5,)),
        ],
        compiler_params=pltpu.CompilerParams(vmem_limit_bytes=SMALL_VMEM),
        cost_estimate=pl.CostEstimate(
            flops=10_000_000_000, bytes_accessed=2 * rows * width, transcendentals=0
        ),
        name="velocity",
    )(in_hbm(hidden), in_hbm(proj_turned))


def prepare_kernel(
    total_blocks,
    step_ref,
    back_hbm,
    ahead_hbm,
    latent_w_hbm,
    prompt_w_hbm,
    time_w_ref,
    qkv_ref,
    mixed_ref,
    keyed_ref,
    gram_ref,
    embed_ref,
    gate_ref,
    bias_ref,
    delta_ref,
    left_ref,
    back_ref,
    ahead_ref,
    latent_w_ref,
    prompt_w_ref,
    sems,
):
    mel, width = latent_w_ref.shape
    small = [
        pltpu.make_async_copy(source, target, sems.at[index])
        for index, (source, target) in enumerate(
            [
                (latent_w_hbm, latent_w_ref),
                (prompt_w_hbm, prompt_w_ref),
                (back_hbm, back_ref),
                (ahead_hbm, ahead_ref),
            ]
        )
    ]
    parts = 3
    columns = 3 * width // parts
    for copy in small:
        copy.start()

    small[0].wait()
    small[1].wait()
    both = jnp.concatenate([latent_w_ref[...], prompt_w_ref[...]], axis=0)
    wide = both.astype(F32)
    centered = wide - jnp.mean(wide, axis=-1, keepdims=True)
    embed = jnp.concatenate(
        [both, latent_w_ref[...], jnp.zeros((256 - 3 * mel, width), BF16)], axis=0
    )
    embed_ref[...] = embed
    col = jnp.mean(embed.astype(F32), axis=-1, keepdims=True)
    row = mm_nt(jnp.ones((16, width), BF16), embed)[0:1] / width
    gram = mm_nt(embed, embed) / width - col * row
    gram_high = gram.astype(BF16)
    gram_ref[0:256] = gram_high
    gram_ref[256:512] = (gram - gram_high.astype(F32)).astype(BF16)

    step = jnp.full((1, time_w_ref.shape[0]), step_ref[0], jnp.int32).astype(F32)
    feats = jnp.broadcast_to(time_features(step), (16, step.shape[1]))
    step = step[:, :128]
    delta_ref[...] = time_value(step + 1.0) - time_value(step)
    high = feats.astype(BF16)
    rest = feats - high.astype(F32)
    mid = rest.astype(BF16)
    low = (rest - mid.astype(F32)).astype(BF16)
    pieces = mm(jnp.concatenate([high, mid, low], axis=0), time_w_ref[...])
    mod = pieces[0:1] + (pieces[16:17] + pieces[32:33])
    shift, scale, gate = mod[:, :width], mod[:, width : 2 * width], mod[:, 2 * width :]
    gate_ref[...] = gate
    left_ref[0 : 2 * mel] = (centered * (1.0 + scale)).astype(BF16)
    shift_high = shift.astype(BF16).astype(F32)
    which = lax.broadcasted_iota(jnp.int32, (16, width), 0)
    left_ref[2 * mel : 2 * mel + 16] = jnp.where(
        which == 0, shift_high, jnp.where(which == 1, shift - shift_high, 0.0)
    ).astype(BF16)

    small[2].wait()
    small[3].wait()
    half, _, span = location()
    per_half = back_ref.shape[0] // 2
    keys = bias_ref.shape[1]
    row_block = lax.broadcasted_iota(jnp.int32, (16, keys), 0)
    lower = jnp.zeros((16, keys), jnp.int32)
    upper = jnp.zeros((16, keys), jnp.int32)
    for block in range(per_half):
        lower = jnp.where(row_block == block, block - back_ref[half * per_half + block], lower)
        upper = jnp.where(row_block == block, block + ahead_ref[half * per_half + block], upper)
    key_block = lax.broadcasted_iota(jnp.int32, (16, keys), 1) // BLK - HALO // BLK
    place = key_block + span * per_half
    seen = (key_block >= lower) & (key_block <= upper) & (place >= 0) & (place < total_blocks)
    bias_ref[0:16] = jnp.where(seen, 0.0, MASKED).astype(BF16)
    bias_ref[16:128] = jnp.zeros((112, keys), BF16)

    left = left_ref[...]
    for part in range(parts):
        start = part * columns
        acc = mm(left, qkv_ref[:, start : start + columns])
        if start < width:
            acc = acc * (math.log2(math.e) / math.sqrt(width // HEADS))
        offset = acc[2 * mel : 2 * mel + 1] + acc[2 * mel + 1 : 2 * mel + 2]
        offset_high = offset.astype(BF16).astype(F32)
        which = lax.broadcasted_iota(jnp.int32, (256 - 3 * mel, columns), 0)
        last = jnp.where(which == 0, offset_high, jnp.where(which == 1, offset - offset_high, 0.0))
        block = jnp.concatenate([acc[: 2 * mel], acc[:mel], last], axis=0).astype(BF16)
        if start < width:
            mixed_ref[:, start : start + columns] = block
        elif start < 2 * width:
            keyed_ref[start - width : start - width + columns] = block.T
        else:
            mixed_ref[:, start - width : start - width + columns] = block


def prepare_call(
    total_blocks, step_index, back, ahead, latent_weight, prompt_weight, time_weight, qkv_weight
):
    mel, width = latent_weight.shape
    return pl.pallas_call(
        functools.partial(prepare_kernel, total_blocks),
        in_specs=[whole(pltpu.SMEM)] + [whole(pltpu.HBM)] * 4 + [whole()] * 2,
        out_specs=[whole()] * 7,
        out_shape=[
            jax.ShapeDtypeStruct((256, 2 * width), BF16),
            jax.ShapeDtypeStruct((width, 256), BF16),
            jax.ShapeDtypeStruct((512, 256), BF16),
            jax.ShapeDtypeStruct((256, width), BF16),
            jax.ShapeDtypeStruct((1, width), F32),
            jax.ShapeDtypeStruct((128, 512 + 2 * HALO), BF16),
            jax.ShapeDtypeStruct((1, 128), F32),
        ],
        scratch_shapes=[
            pltpu.VMEM((2 * mel + 16, width), BF16),
            pltpu.SMEM(back.shape, jnp.int32),
            pltpu.SMEM(ahead.shape, jnp.int32),
            pltpu.VMEM(latent_weight.shape, BF16),
            pltpu.VMEM(prompt_weight.shape, BF16),
            pltpu.SemaphoreType.DMA((4,)),
        ],
        compiler_params=pltpu.CompilerParams(vmem_limit_bytes=VMEM_LIMIT),
        cost_estimate=pl.CostEstimate(
            flops=2 * 256 * width * 3 * width, bytes_accessed=8 * width * width, transcendentals=0
        ),
        name="prepare",
    )(
        step_index,
        in_hbm(back),
        in_hbm(ahead),
        in_hbm(latent_weight),
        in_hbm(prompt_weight),
        time_weight,
        qkv_weight,
    )


def weights_of(delta_ref):
    branch = lax.axis_index("cfg") % 2
    delta = delta_ref[0:1, 0:1]
    mine = jnp.where(branch == 0, 1.0 + GUIDE, -GUIDE) * delta
    other = jnp.where(branch == 0, -GUIDE, 1.0 + GUIDE) * delta
    return mine, other


def updated_end(refs, half, own, whole_block):
    delta_ref, vel_ref, partner_ref, latent_ref = refs

    def ends(ref, places):
        head, tail = places
        return jnp.where(half == 0, ref[:, head : head + HALO], ref[:, tail : tail + HALO])

    mine, other = weights_of(delta_ref)
    return (
        ends(latent_ref, whole_block)
        + (mine * ends(vel_ref, own) + other * ends(partner_ref, own).astype(F32))
    ).astype(BF16)


def far_kernel(delta_ref, vel_ref, partner_ref, latent_ref, prompt_ref, far_ref):
    half, _, _ = location()
    mel, frames = vel_ref.shape
    last = 2 * frames - HALO
    far_ref[0:mel] = updated_end(
        (delta_ref, vel_ref, partner_ref, latent_ref), half, (0, frames - HALO), (0, last)
    )
    far_ref[mel : 2 * mel] = jnp.where(
        half == 0, prompt_ref[:, :HALO], prompt_ref[:, last:]
    ).astype(BF16)


def combine_kernel(
    delta_ref, vel_ref, partner_ref, latent_ref, prompt_ref, next_ref, rows_ref, cross_ref
):
    half, branch, _ = location()
    mel, frames = vel_ref.shape
    mine, other = weights_of(delta_ref)
    latent = jnp.where(half == 0, latent_ref[:, :frames], latent_ref[:, frames:])
    prompt = jnp.where(half == 0, prompt_ref[:, :frames], prompt_ref[:, frames:])
    updated = latent + (mine * vel_ref[...] + other * partner_ref[...].astype(F32))
    head, tail = updated[:, :HALO], updated[:, frames - HALO :]
    cross_ref[...] = jnp.where(half == 0, tail, head).astype(BF16)
    share = frames // 2
    next_ref[...] = jnp.where(branch == 0, updated[:, :share], updated[:, share:])
    high = updated.astype(BF16)
    rows_ref[0:mel] = high
    rows_ref[mel : 2 * mel] = jnp.where(branch == 0, prompt, 0.0).astype(BF16)
    rows_ref[2 * mel : 3 * mel] = (updated - high.astype(F32)).astype(BF16)
    rows_ref[3 * mel : 256] = jnp.zeros((256 - 3 * mel, frames), BF16)


def combine_call(delta, vel, partner, latent, prompt):
    mel, frames = vel.shape
    return pl.pallas_call(
        combine_kernel,
        in_specs=[whole()] * 5,
        out_specs=[whole()] * 3,
        out_shape=[
            jax.ShapeDtypeStruct((mel, frames // 2), F32),
            jax.ShapeDtypeStruct((256, frames), BF16),
            jax.ShapeDtypeStruct((mel, HALO), BF16),
        ],
        compiler_params=pltpu.CompilerParams(vmem_limit_bytes=SMALL_VMEM),
        cost_estimate=pl.CostEstimate(
            flops=5_000_000_000, bytes_accessed=1_000_000, transcendentals=0
        ),
        name="combine",
    )(delta, vel, partner, latent, prompt)


def far_call(delta, vel, partner, latent, prompt):
    return pl.pallas_call(
        far_kernel,
        in_specs=[whole()] * 5,
        out_specs=whole(),
        out_shape=jax.ShapeDtypeStruct((2 * vel.shape[0], HALO), BF16),
        compiler_params=pltpu.CompilerParams(vmem_limit_bytes=SMALL_VMEM),
        name="far",
    )(delta, vel, partner, latent, prompt)


def normalised(rows, gram_ref, mel):
    weighted = mm(gram_ref[0:256], rows) + mm(gram_ref[256:512], rows)
    rows = rows.astype(F32)
    spread = jnp.sum(weighted * rows, axis=0, keepdims=True)
    inverse = lax.rsqrt(jnp.maximum(spread, 0.0) + EPS)
    latent = (rows[0:mel] + rows[2 * mel : 3 * mel]) * inverse
    high = latent.astype(BF16)
    which = lax.broadcasted_iota(jnp.int32, (256 - 3 * mel, rows.shape[1]), 0)
    return jnp.concatenate(
        [
            high,
            (rows[mel : 2 * mel] * inverse).astype(BF16),
            (latent - high.astype(F32)).astype(BF16),
            jnp.where(which < 2, 1.0, 0.0).astype(BF16),
        ],
        axis=0,
    )


def split_values(values, start, value_ref):
    left = lax.broadcasted_iota(jnp.int32, (values.shape[0], 128), 1) < 64
    for part in range(values.shape[1] // 128):
        pair = values[:, 128 * part : 128 * (part + 1)]
        at = 2 * start + 256 * part
        value_ref[:, at : at + 128] = jnp.where(left, pair, 0.0).astype(BF16)
        value_ref[:, at + 128 : at + 256] = jnp.where(left, 0.0, pair).astype(BF16)


def pair_queries(query, tile):
    row = lax.broadcasted_iota(jnp.int32, (TILE, 128), 0)
    lane = lax.broadcasted_iota(jnp.int32, (TILE, 128), 1)
    chosen = (lane == tile * (TILE // BLK) + row // BLK).astype(F32).astype(BF16)
    return jnp.concatenate([query, chosen], axis=1)


def pair_scores(queries, key_left, key_right, bias):
    gap = jnp.zeros_like(key_left)
    key = jnp.concatenate(
        [
            jnp.concatenate([key_left, gap, bias], axis=0),
            jnp.concatenate([gap, key_right, bias], axis=0),
        ],
        axis=1,
    )
    return mm(queries, key)


def pair_sums(scores, value_left, value_right):
    left = lax.broadcasted_iota(jnp.int32, value_left.shape, 1) < 64
    ones_left = jnp.where(left, 1.0, 0.0).astype(BF16)
    ones_right = jnp.where(left, 0.0, 1.0).astype(BF16)
    value = jnp.concatenate(
        [
            jnp.concatenate([value_left, ones_left], axis=1),
            jnp.concatenate([value_right, ones_right], axis=1),
        ],
        axis=0,
    )
    return mm(jnp.exp2(scores).astype(BF16), value)


def less_top(scores, tops):
    size = scores.shape[1] // 2
    return jnp.concatenate([scores[:, :size] - tops[0], scores[:, size:] - tops[1]], axis=1)


def top_of(scores):
    size = scores.shape[1] // 2
    return (
        jnp.max(scores[:, :size], axis=-1, keepdims=True),
        jnp.max(scores[:, size:], axis=-1, keepdims=True),
    )


def in_range(least, most):
    return (jnp.min(least) > SMALL) & (jnp.max(most) < LARGE)


def pair_keys(key_ref, pair, window):
    return (
        key_ref[pl.ds(pair * 128, 64), window],
        key_ref[pl.ds(pair * 128 + 64, 64), window],
    )


def pair_values(value_ref, pair, window):
    return (
        value_ref[window, pl.ds(pair * 256, 128)],
        value_ref[window, pl.ds(pair * 256 + 128, 128)],
    )


def edges_of(frames):
    own = TILE + HALO
    return (
        (0, 0, 0, HALO, 0),
        (frames // TILE - 1, frames - own, HALO, frames + HALO - own, frames + HALO),
    )


def layer_kernel(
    mel,
    share_ref,
    own_ref,
    mixed_ref,
    keyed_ref,
    gram_ref,
    bias_ref,
    embed_ref,
    gate_ref,
    out_w_ref,
    latent_ref,
    query_ref,
    key_ref,
    value_ref,
    done_ref,
    first_ref,
    sums_ref,
    totals_ref,
    context_ref,
    sems,
):
    share = pltpu.make_async_copy(share_ref, latent_ref, sems.at[0])
    share.start()
    frames, width = query_ref.shape
    pairs = width // 128
    own = own_ref[...]
    normed = normalised(own, gram_ref, mel)
    turned = normed.T
    for start in range(0, width, 256):
        cols = slice(start, start + 256)
        key_ref[cols] = mm(keyed_ref[cols], normed).astype(BF16)
        query_ref[:, cols] = mm(turned, mixed_ref[:, cols]).astype(BF16)
        split_values(
            mm(turned, mixed_ref[:, width + start : width + start + 256]), start, value_ref
        )

    def attend(tile, pair, stable):
        at = tile * TILE
        cols = pl.ds(pair * 128, 128)
        window = pl.ds(at - HALO, TILE + 2 * HALO)
        queries = pair_queries(query_ref[pl.ds(at, TILE), cols], tile)
        scores = pair_scores(
            queries, *pair_keys(key_ref, pair, window), bias_ref[:, pl.ds(at, TILE + 2 * HALO)]
        )
        if stable:
            scores = less_top(scores, top_of(scores))
        sums = pair_sums(scores, *pair_values(value_ref, pair, window))
        total = sums[:, 128:]
        context_ref[pl.ds(at - HALO, TILE), cols] = (sums[:, :128] / total).astype(BF16)
        return total

    first, last = HALO // TILE, (frames - HALO) // TILE
    least = jnp.full((TILE, 128), 1.0, F32)
    most = jnp.full((TILE, 128), 1.0, F32)
    for tile in range(first, last):
        for pair in range(pairs):
            total = attend(tile, pair, False)
            least = jnp.minimum(least, total)
            most = jnp.maximum(most, total)
    for edge, (tile, at, _, bias_at, _) in enumerate(edges_of(frames)):
        window = pl.ds(at, TILE + HALO)
        here = slice(edge * TILE, (edge + 1) * TILE)
        for pair in range(pairs):
            cols = slice(pair * 128, (pair + 1) * 128)
            queries = pair_queries(query_ref[tile * TILE : (tile + 1) * TILE, cols], tile)
            scores = pair_scores(
                queries,
                *pair_keys(key_ref, pair, window),
                bias_ref[:, bias_at : bias_at + TILE + HALO],
            )
            sums = pair_sums(scores, *pair_values(value_ref, pair, window))
            sums_ref[here, cols] = sums[:, :128]
            totals_ref[here, cols] = sums[:, 128:]

    def project():
        own_turned = own_ref[...].T
        for start in range(0, width, 512):
            cols = slice(start, start + 512)
            start_rows = mm(own_turned, embed_ref[:, cols])
            projected = mm(context_ref[...], out_w_ref[:, cols])
            done_ref[:, cols] = (
                start_rows[HALO : frames - HALO] + gate_ref[:, cols] * projected
            ).astype(BF16)
            first_ref[0:HALO, cols] = start_rows[0:HALO]
            first_ref[HALO : 2 * HALO, cols] = start_rows[frames - HALO :]

    project()

    @pl.when(jnp.logical_not(in_range(least, most)))
    def _():
        def one(index, carry):
            attend(first + index // pairs, index % pairs, True)
            return carry

        lax.fori_loop(0, (last - first) * pairs, one, 0)
        project()

    share.wait()


def layer_call(share, own, mixed, keyed, gram, bias, embed, gate, out_w):
    mel, frames = share.shape[0], own.shape[1]
    width = out_w.shape[0]
    return pl.pallas_call(
        functools.partial(layer_kernel, mel),
        in_specs=[whole()] * 9,
        out_specs=[whole(pltpu.HBM)] + [whole()] * 7,
        out_shape=[
            jax.ShapeDtypeStruct(share.shape, F32),
            jax.ShapeDtypeStruct((frames, width), BF16),
            jax.ShapeDtypeStruct((width, frames), BF16),
            jax.ShapeDtypeStruct((frames, 2 * width), BF16),
            jax.ShapeDtypeStruct((frames - 2 * HALO, width), BF16),
            jax.ShapeDtypeStruct((2 * HALO, width), F32),
            jax.ShapeDtypeStruct((2 * TILE, width), F32),
            jax.ShapeDtypeStruct((2 * TILE, width), F32),
        ],
        scratch_shapes=[
            pltpu.VMEM((frames - 2 * HALO, width), BF16),
            pltpu.SemaphoreType.DMA((1,)),
        ],
        compiler_params=pltpu.CompilerParams(vmem_limit_bytes=VMEM_LIMIT),
        cost_estimate=pl.CostEstimate(
            flops=5_000_000_000, bytes_accessed=6_000_000, transcendentals=2_000_000
        ),
        name="layer",
    )(share, own, mixed, keyed, gram, bias, embed, gate, out_w)


def close_kernel(
    far_ref,
    cross_ref,
    prompt_ref,
    mixed_ref,
    keyed_ref,
    gram_ref,
    bias_ref,
    query_ref,
    key_ref,
    value_ref,
    sums_ref,
    totals_ref,
    first_ref,
    gate_ref,
    out_w_ref,
    done_ref,
    next_ref,
    near_key_ref,
    near_value_ref,
    context_ref,
    edge_ref,
    sems,
):
    half, branch, _ = location()
    frames, width = query_ref.shape
    pairs = width // 128
    mel = cross_ref.shape[0]
    inner = pltpu.make_async_copy(done_ref, next_ref.at[pl.ds(HALO, frames - 2 * HALO)], sems.at[0])
    inner.start()
    flag = jnp.where(branch == 0, 1.0, 0.0)
    prompt = jnp.where(
        half == 0, prompt_ref[:, frames : frames + HALO], prompt_ref[:, frames - HALO : frames]
    )
    blank = jnp.zeros((256 - 2 * mel, HALO), F32)
    far = far_ref[...].astype(F32)
    cross_rows = jnp.concatenate([cross_ref[...].astype(F32), prompt * flag, blank], axis=0)
    seq_rows = jnp.concatenate([far[0:mel], far[mel:] * flag, blank], axis=0)
    before = jnp.where(half == 0, seq_rows, cross_rows).astype(BF16)
    after = jnp.where(half == 0, cross_rows, seq_rows).astype(BF16)
    normed = normalised(jnp.concatenate([before, after], axis=1), gram_ref, mel)
    turned = normed.T
    for start in range(0, width, 512):
        cols = slice(start, start + 512)
        near_key_ref[cols] = mm(keyed_ref[cols], normed).astype(BF16)
        split_values(
            mm(turned, mixed_ref[:, width + start : width + start + 512]), start, near_value_ref
        )

    edges = edges_of(frames)
    least = jnp.full((TILE, 128), 1.0, F32)
    most = jnp.full((TILE, 128), 1.0, F32)
    for pair in range(pairs):
        cols = slice(pair * 128, (pair + 1) * 128)
        for edge, (tile, _, near_at, _, bias_at) in enumerate(edges):
            window = pl.ds(near_at, HALO)
            here = slice(edge * TILE, (edge + 1) * TILE)
            queries = pair_queries(query_ref[tile * TILE : (tile + 1) * TILE, cols], tile)
            scores = pair_scores(
                queries,
                *pair_keys(near_key_ref, pair, window),
                bias_ref[:, bias_at : bias_at + HALO],
            )
            sums = pair_sums(scores, *pair_values(near_value_ref, pair, window))
            total = sums[:, 128:] + totals_ref[here, cols]
            context_ref[here, cols] = ((sums[:, :128] + sums_ref[here, cols]) / total).astype(BF16)
            least = jnp.minimum(least, total)
            most = jnp.maximum(most, total)

    columns = 256
    copies = []
    for start in range(0, width, columns):
        for edge, row in enumerate((0, frames - HALO)):
            cols = pl.ds(start, columns)
            copies.append(
                pltpu.make_async_copy(
                    edge_ref.at[pl.ds(edge * HALO, HALO), cols],
                    next_ref.at[pl.ds(row, HALO), cols],
                    sems.at[1 + len(copies)],
                )
            )

    def finish():
        for index, start in enumerate(range(0, width, columns)):
            cols = slice(start, start + columns)
            projected = mm(context_ref[...], out_w_ref[:, cols])
            edge_ref[:, cols] = (first_ref[:, cols] + gate_ref[:, cols] * projected).astype(BF16)
            copies[2 * index].start()
            copies[2 * index + 1].start()

    def settle():
        for copy in copies:
            copy.wait()

    finish()

    @pl.when(jnp.logical_not(in_range(least, most)))
    def _():
        settle()
        for edge, (tile, at, near_at, bias_own, bias_near) in enumerate(edges):
            here = slice(edge * TILE, (edge + 1) * TILE)

            def one(pair, carry):
                cols = pl.ds(pair * 128, 128)
                own_window = pl.ds(at, TILE + HALO)
                near_window = pl.ds(near_at, HALO)
                queries = pair_queries(query_ref[tile * TILE : (tile + 1) * TILE, cols], tile)
                own_scores = pair_scores(
                    queries,
                    *pair_keys(key_ref, pair, own_window),
                    bias_ref[:, bias_own : bias_own + TILE + HALO],
                )
                near_scores = pair_scores(
                    queries,
                    *pair_keys(near_key_ref, pair, near_window),
                    bias_ref[:, bias_near : bias_near + HALO],
                )
                tops = [
                    jnp.maximum(a, b) for a, b in zip(top_of(own_scores), top_of(near_scores))
                ]
                sums = pair_sums(
                    less_top(own_scores, tops), *pair_values(value_ref, pair, own_window)
                ) + pair_sums(
                    less_top(near_scores, tops), *pair_values(near_value_ref, pair, near_window)
                )
                context_ref[here, cols] = (sums[:, :128] / sums[:, 128:]).astype(BF16)
                return carry

            lax.fori_loop(0, pairs, one, 0)

        finish()

    inner.wait()
    settle()


def close_call(
    far, cross, prompt, mixed, keyed, gram, bias, query, key, value, sums, totals, first, gate, out_w, done
):
    frames, width = query.shape
    return pl.pallas_call(
        close_kernel,
        in_specs=[whole()] * 16,
        out_specs=whole(pltpu.HBM),
        out_shape=jax.ShapeDtypeStruct((frames, width), BF16),
        scratch_shapes=[
            pltpu.VMEM((width, 2 * HALO), BF16),
            pltpu.VMEM((2 * HALO, 2 * width), BF16),
            pltpu.VMEM((2 * TILE, width), BF16),
            pltpu.VMEM((2 * TILE, width), BF16),
            pltpu.SemaphoreType.DMA((9,)),
        ],
        compiler_params=pltpu.CompilerParams(vmem_limit_bytes=VMEM_LIMIT),
        cost_estimate=pl.CostEstimate(
            flops=2_000_000_000, bytes_accessed=6_000_000, transcendentals=1_000_000
        ),
        name="close",
    )(
        far,
        cross,
        prompt,
        mixed,
        keyed,
        gram,
        bias,
        query,
        key,
        value,
        sums,
        totals,
        first,
        gate,
        out_w,
        done,
    )


def body(
    hidden,
    latent,
    prompt_mel,
    window_back,
    window_ahead,
    step_index,
    proj_weight,
    latent_weight,
    prompt_weight,
    time_weight,
    qkv_weight,
    attn_out_weight,
):
    axes = ("seq", "cfg")
    spans = lax.axis_size("seq")
    total_blocks = 2 * spans * (hidden.shape[0] // BLK)

    def at(span, cell):
        return span * 4 + cell

    everyone = [(span, cell) for span in range(spans) for cell in range(4)]
    to_partner = [(at(s, c), at(s, c ^ 1)) for s, c in everyone]
    to_half = [(at(s, c), at(s, c ^ 3)) for s, c in everyone]
    to_span = [
        (at(s, c), at(s + (1 if c >= 2 else -1), c ^ 3))
        for s, c in everyone
        if 0 <= s + (1 if c >= 2 else -1) < spans
    ]
    vel, sent = velocity_call(hidden, proj_weight.T)
    sent, step_index = lax.optimization_barrier((sent, step_index))
    partner = lax.ppermute(sent, axes, to_partner)
    mixed, keyed, gram, embed, gate, bias, delta = prepare_call(
        total_blocks,
        step_index,
        window_back,
        window_ahead,
        latent_weight,
        prompt_weight,
        time_weight,
        qkv_weight,
    )
    far = far_call(delta, vel, partner, latent, prompt_mel)
    far = lax.ppermute(far, axes, to_span)
    share, own, cross = combine_call(delta, vel, partner, latent, prompt_mel)
    cross = lax.ppermute(cross, axes, to_half)
    latent_out, query, key, value, done, first, sums, totals = layer_call(
        share, own, mixed, keyed, gram, bias, embed, gate, attn_out_weight
    )
    hidden_next = close_call(
        far,
        cross,
        prompt_mel,
        mixed,
        keyed,
        gram,
        bias,
        query,
        key,
        value,
        sums,
        totals,
        first,
        gate,
        attn_out_weight,
        done,
    )
    return (latent_out, hidden_next)


def solution(mesh):
    in_specs = (
        P(("seq", "cfg"), None),
        P(None, "seq"),
        P(None, "seq"),
        P("seq"),
        P("seq"),
        P(),
        P(),
        P(),
        P(),
        P(),
        P(),
        P(),
    )
    out_specs = (P(None, ("seq", "cfg")), P(("seq", "cfg"), None))
    return jax.shard_map(body, mesh=mesh, in_specs=in_specs, out_specs=out_specs, check_vma=False)
```
